512 devices in a mesh: gx: 16 (over x, y_lo), gy: 32 (over y_hi, z, core).
Axes of the slice: x: 4, y: 8 (y_hi: 2, y_lo: 4; y = y_hi * 4 + y_lo), z: 8, core: 2. Of those that a mesh axis runs over, the one named last changes fastest.
Arguments:
- start_block: float32 [16, 16, 32, 64, 128], P(None, 'gx', 'gy'), may hold values from -4 to 4
- labels: int32 [16, 32, 64, 128], P('gx', 'gy'), may hold values from -8 to 15
- materials: int32 [16, 32, 128], P('gx', 'gy'), may hold values from 0 to 7
- mat_scales: float32 [8], replicated, may hold values from 0.01 to 0.1
- cell_stiffness: float32 [125, 125], replicated, may hold values from -16 to 16, as said below
Outputs:
- solution: float32 [16, 16, 32, 64, 128], P(None, 'gx', 'gy')
- residual: float32 [16, 16, 32, 64, 128], P(None, 'gx', 'gy')
The draws below stay inside these ranges and needn't reach their ends.
Inputs may be any that keep to these rules, and one draw needn't show every extreme that they name: `labels`: a label c of 0 or more puts the node on conductor c; a negative label puts it on none. `materials`: an index into mat_scales. `cell_stiffness`: symmetric positive semidefinite, every row sums to zero.
All inputs are finite; a program needn't handle non-finite values.
Results may differ from the reference program's by a relative error of at most 0.002.
Values sent between devices are 32-bit elements; how exact they have to be, the bound alone decides.
A program may use at most 64 MiB of HBM per device.

```python
import math
import jax
import jax.numpy as jnp
import numpy as np
from jax import lax

COLS = 16
CELL_NODES = 125
MATS = 8
ITERS = 4
EZ = 128
EX = 16
EY = 32


def line_tables():
    points = np.array([-1.0, -np.sqrt(3.0 / 7.0), 0.0, np.sqrt(3.0 / 7.0), 1.0])
    quad_weights = np.array([0.1, 49.0 / 90.0, 32.0 / 45.0, 49.0 / 90.0, 0.1])
    legendre = (35.0 * points ** 4 - 30.0 * points ** 2 + 3.0) / 8.0
    derivative = np.zeros((5, 5))
    identity = np.zeros((5, 5))
    for row in range(5):
        identity[row, row] = 1.0
        for column in range(5):
            if row != column:
                derivative[row, column] = legendre[row] / (legendre[column] * (points[row] - points[column]))
    derivative[0, 0] = -5.0
    derivative[4, 4] = 5.0
    stiff_line = derivative.T * quad_weights[None, :] @ derivative
    row_sums = stiff_line.sum(1)
    stiff_line = stiff_line - identity * row_sums[:, None]
    stiff_line = 0.5 * (stiff_line + stiff_line.T)
    mass_line = identity * quad_weights[:, None]
    return (stiff_line.astype(np.float32), mass_line.astype(np.float32))


def draw_cell_stiffness(key, part):
    key = jax.random.fold_in(key, 11)
    factors = jax.random.uniform(key, (3,), jnp.float32, 0.5, 1.5)
    stiff_np, mass_np = line_tables()
    stiff_line = jnp.asarray(stiff_np)
    mass_line = jnp.asarray(mass_np)
    along_x = stiff_line[:, None, None, :, None, None] * mass_line[None, :, None, None, :, None] * mass_line[None, None, :, None, None, :]
    along_y = mass_line[:, None, None, :, None, None] * stiff_line[None, :, None, None, :, None] * mass_line[None, None, :, None, None, :]
    along_z = mass_line[:, None, None, :, None, None] * mass_line[None, :, None, None, :, None] * stiff_line[None, None, :, None, None, :]
    total = factors[0] * along_x + factors[1] * along_y + factors[2] * along_z
    return total.reshape(CELL_NODES, CELL_NODES)


def place_ends(values, own_key, smallest, largest):
    longest = values.shape.index(max(values.shape))
    spots = []
    for shift in (0, 1):
        where = [jax.random.randint(jax.random.fold_in(own_key, axis), (), 0, length) for axis, length in enumerate(values.shape)]
        where[longest] = (where[longest] + shift) % values.shape[longest]
        spots.append(tuple(where))
    return values.at[spots[0]].set(smallest).at[spots[1]].set(largest)


def level_of(key, dims, cuts, smallest, top_value):
    def one(position, parts):
        draws = jax.random.uniform(jax.random.fold_in(jax.random.fold_in(key, 6), position), (parts,), jnp.float32, smallest / len(cuts), top_value / len(cuts))
        return jnp.repeat(jnp.exp(draws), dims[position] // parts).reshape((-1,) + (1,) * (len(dims) - position - 1))

    gain = one(*cuts[0])
    for cut in cuts[1:]:
        gain = gain * one(*cut)
    return gain


def normal_values(stream_key, extent, spread, bound, cuts=(), held_as=jnp.bfloat16):
    factor_of = level_of(stream_key, extent, cuts, -0.22, 0.18) if cuts else 1.0
    result = jax.random.normal(stream_key, extent, jnp.float32) * spread * factor_of
    return jnp.minimum(jnp.maximum(result, -bound), bound).astype(held_as)


def setup_inputs(seed: int = 0) -> dict:
    key_list = jax.random.split(jax.random.key(seed), 6)
    start_block = normal_values(key_list[0], (COLS, EX, EY, 64, EZ), 0.5, 4.0, ((1, 16), (2, 32)), jnp.float32)
    labels = place_ends(jax.random.randint(key_list[1], (EX, EY, 64, EZ), -8, 16), jax.random.fold_in(key_list[1], 1), -8, 15).astype(jnp.int32)
    materials = place_ends(jax.random.randint(key_list[2], (EX, EY, EZ), 0, MATS), jax.random.fold_in(key_list[2], 1), 0, MATS - 1).astype(jnp.int32)
    mat_scales = jnp.clip(jnp.exp(jax.random.uniform(key_list[3], (MATS,), jnp.float32, math.log(0.01), math.log(0.1))), 0.01, 0.1)
    cell_stiffness = draw_cell_stiffness(jax.random.fold_in(key_list[5], 71), 0)
    return dict(start_block=start_block, labels=labels, materials=materials, mat_scales=mat_scales, cell_stiffness=cell_stiffness)


PENALTY = 1.0

def next_plane(values):
    return jnp.concatenate([values[..., 1:], jnp.zeros_like(values[..., :1])], -1)

def prev_plane(values):
    return jnp.concatenate([jnp.zeros_like(values[..., :1]), values[..., :-1]], -1)

def assemble(wider, next_rows):
    slabs = []
    for along_x in range(5):
        for along_y in range(5):
            if along_y < 4:
                start = 16 * along_x + 4 * along_y
                four = wider[..., start:start + 4, :]
            else:
                four = next_rows[..., 4 * along_x:4 * along_x + 4, :]
            slabs.append(four)
            slabs.append(next_plane(four[..., 0:1, :]))
    return jnp.concatenate(slabs, 3)

def contract(expanded, scales, stiffness):
    mapped = jnp.einsum('pq,cijqk->cijpk', stiffness, expanded, precision=lax.Precision.HIGHEST)
    return mapped * scales[None, :, :, None, :]

def fold_planes(mapped):
    slabs = []
    for along_x in range(5):
        for along_y in range(5):
            start = 25 * along_x + 5 * along_y
            four = mapped[..., start:start + 4, :]
            last = mapped[..., start + 4:start + 5, :]
            slabs.append(four[..., 0:1, :] + prev_plane(last))
            slabs.append(four[..., 1:4, :])
    return jnp.concatenate(slabs, 3)

def operate_one(field, mask, scales, stiffness):
    nextx = jnp.roll(field[:, :, :, 0:16], -1, axis=1)
    wider = jnp.concatenate([field, nextx], 3)
    lower = jnp.concatenate([wider[..., 16 * along_x:16 * along_x + 4, :] for along_x in range(5)], 3)
    next_rows = jnp.concatenate([lower[:, :, 1:], jnp.zeros_like(lower[:, :, :1])], 2)
    mapped = contract(assemble(wider, next_rows), scales, stiffness)
    folded = fold_planes(mapped)
    upper = jnp.concatenate([folded[..., 20 * along_x + 16:20 * along_x + 20, :] for along_x in range(5)], 3)
    inner = jnp.concatenate([folded[..., 20 * along_x:20 * along_x + 16, :] for along_x in range(5)], 3)
    moved = jnp.concatenate([jnp.zeros_like(upper[:, :, :1]), upper[:, :, :-1]], 2)
    filler = jnp.zeros_like(inner[..., 0:12, :])
    inner = inner + jnp.concatenate([piece for along_x in range(5) for piece in (moved[..., 4 * along_x:4 * along_x + 4, :], filler)], 3)
    outer = inner[..., 64:80, :]
    core = inner[..., 0:64, :]
    movedx = jnp.roll(outer, 1, axis=1)
    core = core + jnp.concatenate([movedx, jnp.zeros_like(core[..., 16:64, :])], 3)
    return core + PENALTY * mask[None] * field

def operate(block, mask, scales, stiffness):
    return lax.map(lambda field: operate_one(field[None], mask, scales, stiffness)[0], block)

def gram(left, right):
    columns = left.shape[0]
    return jnp.dot(left.reshape(columns, -1), right.reshape(columns, -1).T, precision=lax.Precision.HIGHEST)

def combine(coef, block):
    columns = block.shape[0]
    return jnp.dot(coef.T, block.reshape(columns, -1), precision=lax.Precision.HIGHEST).reshape(block.shape)

def solve_spd(matrix, rhs):
    factor = jnp.linalg.cholesky(matrix)
    return jax.scipy.linalg.cho_solve((factor, True), rhs, check_finite=False)

def reference(start_block, labels, materials, mat_scales, cell_stiffness):
    columns = start_block.shape[0]
    mask = (labels >= 0).astype(start_block.dtype)
    targets = (labels[None] == jnp.arange(columns, dtype=jnp.int32)[:, None, None, None, None]).astype(start_block.dtype)
    scales = jnp.zeros(materials.shape, start_block.dtype)
    for which in range(mat_scales.shape[0]):
        scales = scales + jnp.where(materials == which, mat_scales[which], jnp.zeros_like(scales))
    solution = start_block
    residual = targets - operate(start_block, mask, scales, cell_stiffness)
    direction = residual
    norm_now = gram(residual, residual)
    for step in range(ITERS):
        image = operate(direction, mask, scales, cell_stiffness)
        alpha = solve_spd(gram(direction, image), norm_now)
        solution = solution + combine(alpha, direction)
        residual = residual - combine(alpha, image)
        if step + 1 < ITERS:
            norm_next = gram(residual, residual)
            beta = solve_spd(norm_now, norm_next)
            direction = residual + combine(beta, direction)
            norm_now = norm_next
    return (solution, residual)
```

```python
import functools

import jax
import jax.numpy as jnp
import ml_dtypes
import numpy as np
from jax import lax
from jax.experimental import pallas as pl
from jax.experimental.pallas import tpu as pltpu
from jax.sharding import PartitionSpec as P

COLS = 16
NQ = 4
CQ = COLS // NQ
PENALTY = 1.0
MESH = pl.DeviceIdType.MESH
BF = jnp.bfloat16
F32 = jnp.float32


def node_order():
    rows = [(a, b, d) for a in range(4) for b in range(4) for d in range(4)]
    rows += [(4, b, d) for b in range(4) for d in range(4)]
    rows += [(a, 4, d) for a in range(4) for d in range(4)]
    rows += [(a, b, 4) for a in range(4) for b in range(4)]
    rows += [(4, b, 4) for b in range(4)]
    rows += [(a, 4, 4) for a in range(4)]
    rows += [(4, 4, d) for d in range(5)]
    return [25 * a + 5 * b + d for a, b, d in rows]


def order_matrix():
    out = np.zeros((128, 128), np.float32)
    for row, node in enumerate(node_order()):
        out[row, node] = 1.0
    return out.astype(ml_dtypes.bfloat16)


def moment_tables():
    mu = np.zeros((8, 8))
    for k in range(4):
        mu[k, k] = 1.0
    mu[4, 4] = 1.0
    for i in (1, 2, 3):
        mu[4 + i, 4 + i] = 2.0
        mu[4 + i] -= mu[4 - i]

    def inner(i, j):
        return 0.5 * (mu[i + j] + mu[abs(i - j)])

    tables = np.zeros((3, 4, 8, 8))
    for i in range(4):
        for j in range(4):
            tables[0, i, :, j] = inner(i, j)
            tables[1, i, :, j] = 0.5 * (inner(i, j + 1) + inner(i, abs(j - 1)))
        tables[2, i, :, 4] = inner(i, 0)
    out = np.zeros((128, 3 * 4 * 128), np.float32)
    for which in range(3):
        for i in range(4):
            start = 128 * (4 * which + i)
            out[:, start : start + 128] = np.kron(tables[which, i], np.eye(16))
    return out.astype(ml_dtypes.bfloat16)


def split(value):
    high = value.astype(BF)
    low = (value - high.astype(F32)).astype(BF)
    return high, low


def dot(left, right):
    return jnp.dot(left, right, preferred_element_type=F32)


def dot_t(left, right):
    return lax.dot_general(left, right, (((1,), (1,)), ((), ())), preferred_element_type=F32)


def exact_dot(value, table):
    rows = value.shape[0]
    high = value.astype(BF)
    rest = value - high.astype(F32)
    middle = rest.astype(BF)
    low = (rest - middle.astype(F32)).astype(BF)
    out = dot(jnp.concatenate([high, middle, low], 0), table)
    return out[0:rows] + out[rows : 2 * rows] + out[2 * rows : 3 * rows]


def iota(shape, axis):
    return lax.broadcasted_iota(jnp.int32, shape, axis)


def ones_where(condition):
    return jnp.where(condition, 1.0, 0.0).astype(BF)


def kernel(
    nx, ny, n1,
    x0, lab, mat, ms, kin, order, table,
    xo, ro,
    v, w, rim, corner, ysend, csend, zs, zcs, zr, zcr, tail, kpad, kk, klo, maskb, srow,
    stat, stbuf, gbuf, gm, yst, gres, colr, cs_ref,
    es, er, rs, rr, ss, sr,
):
    gx = lax.axis_index("gx")
    gy = lax.axis_index("gy")
    n3 = ny // n1
    xprev = lax.rem(gx + nx - 1, nx)
    xnext = lax.rem(gx + 1, nx)
    has_prev = gy > 0
    has_next = gy < ny - 1
    yprev = lax.max(gy - 1, 0)
    ynext = lax.min(gy + 1, ny - 1)

    pos1 = lax.rem(gy, n1)
    pos3 = lax.div(gy, n1)
    stages = (
        (0, n1, pos1, lambda p: (gx, gy - pos1 + p)),
        (n1, nx, gx, lambda p: (p, gy)),
        (n1 + nx, n3, pos3, lambda p: (gx, p * n1 + pos1)),
    )

    barrier = pltpu.get_barrier_semaphore()

    def greet(device):
        pl.semaphore_signal(barrier, inc=1, device_id=device, device_id_type=MESH)

    greet((xprev, gy))
    greet((xnext, gy))

    @pl.when(has_prev)
    def _():
        greet((gx, yprev))
        greet((xprev, yprev))

    @pl.when(has_next)
    def _():
        greet((gx, ynext))
        greet((xnext, ynext))

    for _, size, pos, device in stages:
        def hello(i, carry, size=size, pos=pos, device=device):
            greet(device(lax.rem(pos + i, size)))
            return carry

        lax.fori_loop(1, size, hello, 0)

    kpad[...] = jnp.zeros_like(kpad)
    kpad[0:125, 0:125] = kin[...]
    khigh, klow = split(kpad[...])
    pm = order[...]

    def permuted(value):
        return dot_t(dot(pm, value).astype(BF), pm).astype(BF)

    khigh = permuted(khigh)
    kk[:, 0:128] = khigh
    kk[:, 128:256] = khigh
    klo[...] = permuted(klow)
    maskb[...] = jnp.where(lab[...] >= 0, PENALTY, 0.0)
    scale = jnp.zeros((1, 128), F32)
    for which in range(8):
        scale = scale + jnp.where(mat[...] == which, ms[which], 0.0)
    srow[...] = jnp.broadcast_to(scale, (8, 128))
    tail[...] = jnp.zeros_like(tail)

    @pl.when(jnp.logical_not(has_next))
    def _():
        rim[:, :, 16:32, :] = jnp.zeros((NQ, CQ, 16, 128), F32)
        corner[...] = jnp.zeros_like(corner)

    @pl.when(jnp.logical_not(has_prev))
    def _():
        zr[:, :, 16:32, :] = jnp.zeros((NQ, CQ, 16, 128), F32)
        zcr[...] = jnp.zeros_like(zcr)

    def rcopy(src, dst, send, recv, device):
        return pltpu.make_async_remote_copy(
            src_ref=src, dst_ref=dst, send_sem=send, recv_sem=recv, device_id=device, device_id_type=MESH
        )

    def ext(src, q):
        first = pl.ds(0, 16)
        return (
            rcopy(src.at[q, :, first], rim.at[q, :, first], es.at[0, q], er.at[0, q], (xprev, gy)),
            rcopy(ysend.at[q], rim.at[q, :, pl.ds(16, 16)], es.at[1, q], er.at[1, q], (gx, yprev)),
            rcopy(csend.at[q], corner.at[q], es.at[2, q], er.at[2, q], (xprev, yprev)),
        )

    def ret(q):
        first, second = pl.ds(0, 16), pl.ds(16, 16)
        return (
            rcopy(zs.at[q, :, first], zr.at[q, :, first], rs.at[0, q], rr.at[0, q], (xnext, gy)),
            rcopy(zs.at[q, :, second], zr.at[q, :, second], rs.at[1, q], rr.at[1, q], (gx, ynext)),
            rcopy(zcs.at[q], zcr.at[q], rs.at[2, q], rr.at[2, q], (xnext, ynext)),
        )

    def extend_start(src, q):
        for j in range(CQ):
            for a in range(4):
                ysend[q, j, 4 * a : 4 * a + 4, :] = src[q, j, 16 * a : 16 * a + 4, :]
            csend[q, 4 * j : 4 * j + 4, :] = src[q, j, 0:4, :]
        copies = ext(src, q)
        copies[0].start()

        @pl.when(has_prev)
        def _():
            copies[1].start()
            copies[2].start()

    def extend_arrived(src, q):
        copies = ext(src, q)
        copies[0].wait_recv()

        @pl.when(has_next)
        def _():
            copies[1].wait_recv()
            copies[2].wait_recv()

    def extend_sent(src, q):
        copies = ext(src, q)
        copies[0].wait_send()

        @pl.when(has_prev)
        def _():
            copies[1].wait_send()
            copies[2].wait_send()

    def return_start(q):
        copies = ret(q)
        copies[0].start()

        @pl.when(has_next)
        def _():
            copies[1].start()
            copies[2].start()

    def return_arrived(q):
        copies = ret(q)
        copies[0].wait_recv()

        @pl.when(has_prev)
        def _():
            copies[1].wait_recv()
            copies[2].wait_recv()

    def return_sent(q):
        copies = ret(q)
        copies[0].wait_send()

        @pl.when(has_next)
        def _():
            copies[1].wait_send()
            copies[2].wait_send()

    def next_plane(value):
        lane = iota(value.shape, 1)
        return jnp.where(lane == 127, 0.0, pltpu.roll(value, 127, 1))

    def prev_plane(value):
        lane = iota(value.shape, 1)
        return jnp.where(lane == 0, 0.0, pltpu.roll(value, 1, 1))

    def cells(src, q):
        blocks = []
        for j in range(CQ):
            tail[j, 0:4, :] = corner[q, 4 * j : 4 * j + 4, :]
            tail[j, 4:5, :] = next_plane(corner[q, 4 * j : 4 * j + 1, :])
            blocks.append(
                jnp.concatenate(
                    [
                        src[q, j],
                        rim[q, j],
                        next_plane(src[q, j, pl.ds(0, 16, stride=4), :]),
                        next_plane(rim[q, j, pl.ds(0, 8, stride=4), :]),
                        tail[j],
                    ],
                    0,
                )
            )
        high, low = split(jnp.concatenate(blocks, 1))
        mapped = dot(kk[...], jnp.concatenate([high, low], 0)) + dot(klo[...], high)
        scales = srow[0:1, :]
        for j in range(CQ):
            out = mapped[:, 128 * j : 128 * j + 128] * scales
            w[q, j] = out[0:64] + maskb[...] * src[q, j]
            w[q, j, pl.ds(0, 16, stride=4), :] += prev_plane(out[96:112])
            zs[q, j] = out[64:96]
            zs[q, j, pl.ds(0, 8, stride=4), :] += prev_plane(out[112:120])
            zcs[q, 4 * j : 4 * j + 4, :] = out[120:124]
            zcs[q, 4 * j : 4 * j + 1, :] += prev_plane(out[124:125])

    def gather_rims(q):
        for j in range(CQ):
            w[q, j, 0:16, :] += zr[q, j, 0:16, :]
            for a in range(4):
                w[q, j, 16 * a : 16 * a + 4, :] += zr[q, j, 16 + 4 * a : 20 + 4 * a, :]
            w[q, j, 0:4, :] += zcr[q, 4 * j : 4 * j + 4, :]

    def operator(src, number, finish, target):
        def apply(q, carry):
            extend_arrived(src, q)
            if number > 0:
                return_sent(q)
            cells(src, q)
            return_start(q)
            return carry

        lax.fori_loop(0, NQ, apply, 0)
        return functools.partial(_finish, src, number, finish, target)

    def _finish(src, number, finish, target):
        def done(q, carry):
            return_arrived(q)
            extend_sent(src, q)
            gather_rims(q)
            finish(q)
            if number < 4:
                extend_start(target, q)
            return carry

        lax.fori_loop(0, NQ, done, 0)

    def reduce_start(stage, number, buf, value):
        start, size, pos, device = stages[stage]
        buf[start + pos] = value

        def send(i, carry):
            p = lax.rem(pos + i, size)
            here = buf.at[start + pos]
            rcopy(here, here, ss.at[number, start + p], sr.at[number, start + pos], device(p)).start()
            return carry

        lax.fori_loop(1, size, send, 0)

    def reduce_done(stage, number, buf):
        start, size, pos, device = stages[stage]

        def take(i, carry):
            p = lax.rem(pos + i, size)
            here = buf.at[start + p]
            copy = rcopy(here, here, ss.at[number, start + p], sr.at[number, start + p], device(p))
            copy.wait_recv()
            copy.wait_send()
            return carry

        lax.fori_loop(1, size, take, 0)
        total = buf[start]
        for p in range(1, size):
            total = total + buf[start + p]
        return total

    pl.semaphore_wait(
        barrier,
        2 + (n1 - 1) + (nx - 1) + (n3 - 1) + 2 * (gy > 0).astype(jnp.int32) + 2 * (gy < ny - 1).astype(jnp.int32),
    )

    def first(q, carry):
        extend_start(x0, q)
        return carry

    lax.fori_loop(0, NQ, first, 0)

    def finish0(q):
        for j in range(CQ):
            target = jnp.where(lab[...] == CQ * q + j, 1.0, 0.0)
            v[0, q, j] = target - w[q, j]

    operator(x0, 0, finish0, v.at[0])()

    stat[...] = jnp.zeros_like(stat)

    def finish1(q):
        old = v[0, q].reshape(CQ * 8, 8, 128)
        new = w[q].reshape(CQ * 8, 8, 128)
        v[1, q] = w[q]
        stat[0] += jnp.sum(old * old, 0)
        stat[1] += jnp.sum(old * new, 0)
        stat[2] += jnp.sum(new * new, 0)

    operator(v.at[0], 1, finish1, v.at[1])()

    for row in range(3):
        cs_ref[row : row + 1, :] = jnp.sum(stat[row], 0, keepdims=True)
    cs_ref[3:8, :] = jnp.zeros((5, 128), F32)
    reduce_start(0, 0, stbuf, cs_ref[...])
    rest = operator(v.at[1], 2, None, None)
    reduce_start(1, 0, stbuf, reduce_done(0, 0, stbuf))
    reduce_start(2, 0, stbuf, reduce_done(1, 0, stbuf))
    sums = jnp.sum(reduce_done(2, 0, stbuf), 1, keepdims=True)
    theta = sums[1:2] / sums[0:1]
    spread = sums[2:3] / sums[0:1] - theta * theta
    delta = 2.0 * jnp.sqrt(jnp.maximum(spread, 1e-6 * theta * theta))
    colr[0:1, :] = jnp.broadcast_to(theta, (1, 128))
    colr[1:2, :] = jnp.broadcast_to(delta, (1, 128))
    colr[2:3, :] = jnp.broadcast_to(1.0 / delta, (1, 128))

    def finish2(q):
        theta, inverse = colr[0:1, :], colr[2:3, :]
        for j in range(CQ):
            v0, u1 = v[0, q, j], v[1, q, j]
            v1 = (u1 - theta * v0) * inverse
            a1 = (w[q, j] - theta * u1) * inverse
            v[1, q, j] = v1
            v[2, q, j] = 2.0 * (a1 - theta * v1) * inverse - v0

    _finish(v.at[1], 2, finish2, v.at[2])

    def finish_next(number):
        def finish(q):
            theta, inverse = colr[0:1, :], colr[2:3, :]
            for j in range(CQ):
                v[number, q, j] = 2.0 * (w[q, j] - theta * v[number - 1, q, j]) * inverse - v[number - 2, q, j]

        return finish

    operator(v.at[2], 3, finish_next(3), v.at[3])()

    def grouped(number):
        value = v[number]
        return jnp.concatenate(
            [value[:, :, 8 * g : 8 * g + 8, :].reshape(8 * COLS, 128) for g in range(8)], 1
        )

    def grams(number, offset):
        high, low = split(grouped(number))
        yst[0:128, :] = high
        yst[128:256, :] = low

        def one(j, carry):
            high, low = split(grouped(j))
            out = dot_t(jnp.concatenate([high, low], 0), yst[...])
            out = out[0:128, 0:128] + out[0:128, 128:256] + out[128:256, 0:128] + out[128:256, 128:256]
            same = (iota((128, 128), 0) & 7) == (iota((128, 128), 1) & 7)
            out = jnp.sum(jnp.where(same, out, 0.0).reshape(COLS, 8, 128), 1)
            place = ones_where(iota((128, 128), 1) == 16 * (offset + j) + (iota((128, 128), 0) >> 3))
            gres[...] += exact_dot(out, place)
            return carry

        lax.fori_loop(0, 4, one, 0)

    gres[...] = jnp.zeros_like(gres)
    grams(0, 0)
    operator(v.at[3], 4, finish_next(4), None)()
    grams(4, 4)

    reduce_start(0, 1, gbuf, gres[...])
    reduce_start(1, 1, gbuf, reduce_done(0, 1, gbuf))
    reduce_start(2, 1, gbuf, reduce_done(1, 1, gbuf))
    blocks = reduce_done(2, 1, gbuf)

    theta, delta = colr[0:1, :], colr[1:2, :]
    parts = exact_dot(blocks, table[...])
    for i in range(4):
        at = [parts[:, 128 * (4 * which + i) : 128 * (4 * which + i) + 128] for which in range(3)]
        gm[16 * i : 16 * i + 16, :] = theta * at[0] + delta * at[1] + at[2]

    def eliminate(k, carry):
        row = gm[pl.ds(k, 1), :]
        value = gm[...]
        here = iota((64, 128), 1) == k
        col = jnp.sum(jnp.where(here, value, 0.0), 1, keepdims=True)
        pivot = jnp.sum(jnp.where(iota((1, 128), 1) == k, row, 0.0), 1, keepdims=True)
        row = row / pivot
        gm[...] = jnp.where(iota((64, 128), 0) == k, row, value - col * row)
        return carry

    lax.fori_loop(0, 64, eliminate, 0)

    c = [gm[16 * j : 16 * j + 16, :] for j in range(4)]
    half = 0.5 * delta
    unit = jnp.where(iota((16, 128), 0) == iota((16, 128), 1) - 64, 1.0, 0.0)
    e = [
        unit - theta * c[0] - half * c[1],
        -(theta * c[1] + delta * c[0] + half * c[2]),
        -(theta * c[2] + half * (c[1] + c[3])),
        -(theta * c[3] + half * c[2]),
        -(half * c[3]),
    ]
    nothing = jnp.zeros((16, 128), F32)
    forx = jnp.concatenate(c + [nothing] * 4, 0).T
    forr = jnp.concatenate(e + [nothing] * 3, 0).T
    coef = jnp.concatenate([forx[64:80], forr[64:80]], 0)
    spread_in = ones_where((iota((128, 640), 1) >> 3) == iota((128, 640), 0))
    spread_out = ones_where((iota((256, 32), 0) >> 3) == iota((256, 32), 1))
    same = (iota((256, 640), 0) & 7) == (iota((256, 640), 1) & 7)

    def wide(value):
        value = dot(spread_out, dot(value, spread_in).astype(BF))
        return jnp.where(same, value, 0.0).astype(BF)

    chigh, clow = split(coef)
    chigh, clow = wide(chigh), wide(clow)
    for g in range(8):
        field = jnp.concatenate(
            [v[j, :, :, 8 * g : 8 * g + 8, :].reshape(8 * COLS, 128) for j in range(5)], 0
        )
        high, low = split(field)
        out = dot(chigh, high) + dot(chigh, low) + dot(clow, high)
        xo[:, :, 8 * g : 8 * g + 8, :] = x0[:, :, 8 * g : 8 * g + 8, :] + out[0:128].reshape(NQ, CQ, 8, 128)
        ro[:, :, 8 * g : 8 * g + 8, :] = out[128:256].reshape(NQ, CQ, 8, 128)

    for q in range(NQ):
        return_sent(q)


def on_device(start_block, labels, materials, mat_scales, cell_stiffness):
    nx, ny = lax.axis_size("gx"), lax.axis_size("gy")
    n1 = 8 if ny % 8 == 0 else 2
    slots = n1 + nx + ny // n1
    vmem = pl.BlockSpec(memory_space=pltpu.VMEM)
    block = jax.ShapeDtypeStruct((NQ, CQ, 64, 128), F32)
    out = pl.pallas_call(
        functools.partial(kernel, nx, ny, n1),
        out_shape=(block, block),
        in_specs=[vmem, vmem, vmem, pl.BlockSpec(memory_space=pltpu.SMEM), vmem, vmem, vmem],
        out_specs=(vmem, vmem),
        scratch_shapes=[
            pltpu.VMEM((5, NQ, CQ, 64, 128), F32),
            pltpu.VMEM((NQ, CQ, 64, 128), F32),
            pltpu.VMEM((NQ, CQ, 32, 128), F32),
            pltpu.VMEM((NQ, 4 * CQ, 128), F32),
            pltpu.VMEM((NQ, CQ, 16, 128), F32),
            pltpu.VMEM((NQ, 4 * CQ, 128), F32),
            pltpu.VMEM((NQ, CQ, 32, 128), F32),
            pltpu.VMEM((NQ, 4 * CQ, 128), F32),
            pltpu.VMEM((NQ, CQ, 32, 128), F32),
            pltpu.VMEM((NQ, 4 * CQ, 128), F32),
            pltpu.VMEM((CQ, 8, 128), F32),
            pltpu.VMEM((128, 128), F32),
            pltpu.VMEM((128, 256), BF),
            pltpu.VMEM((128, 128), BF),
            pltpu.VMEM((64, 128), F32),
            pltpu.VMEM((8, 128), F32),
            pltpu.VMEM((3, 8, 128), F32),
            pltpu.VMEM((slots, 8, 128), F32),
            pltpu.VMEM((slots, 16, 128), F32),
            pltpu.VMEM((64, 128), F32),
            pltpu.VMEM((256, 1024), BF),
            pltpu.VMEM((16, 128), F32),
            pltpu.VMEM((8, 128), F32),
            pltpu.VMEM((8, 128), F32),
            pltpu.SemaphoreType.DMA((3, NQ)),
            pltpu.SemaphoreType.DMA((3, NQ)),
            pltpu.SemaphoreType.DMA((3, NQ)),
            pltpu.SemaphoreType.DMA((3, NQ)),
            pltpu.SemaphoreType.DMA((2, slots)),
            pltpu.SemaphoreType.DMA((2, slots)),
        ],
        compiler_params=pltpu.CompilerParams(
            collective_id=0, has_side_effects=True, vmem_limit_bytes=48 * 1024 * 1024
        ),
    )(
        start_block.reshape(NQ, CQ, 64, 128),
        labels.reshape(64, 128),
        materials.reshape(1, 128),
        mat_scales,
        cell_stiffness,
        jnp.asarray(order_matrix()),
        jnp.asarray(moment_tables()),
    )
    return tuple(one.reshape(start_block.shape) for one in out)


def solution(mesh):
    spread = P(None, "gx", "gy", None, None)
    return jax.shard_map(
        on_device,
        mesh=mesh,
        in_specs=(spread, P("gx", "gy", None, None), P("gx", "gy", None), P(), P()),
        out_specs=(spread, spread),
        check_vma=False,
    )
```

```python
import functools

import jax
import jax.numpy as jnp
import ml_dtypes
import numpy as np
from jax import lax
from jax.experimental import pallas as pl
from jax.experimental.pallas import tpu as pltpu
from jax.sharding import PartitionSpec as P

COLS = 16
NQ = 4
CQ = COLS // NQ
PENALTY = 1.0
MESH = pl.DeviceIdType.MESH
BF = jnp.bfloat16
F32 = jnp.float32


def node_order():
    rows = [(a, b, d) for a in range(4) for b in range(4) for d in range(4)]
    rows += [(4, b, d) for b in range(4) for d in range(4)]
    rows += [(a, 4, d) for a in range(4) for d in range(4)]
    rows += [(a, b, 4) for a in range(4) for b in range(4)]
    rows += [(4, b, 4) for b in range(4)]
    rows += [(a, 4, 4) for a in range(4)]
    rows += [(4, 4, d) for d in range(5)]
    return [25 * a + 5 * b + d for a, b, d in rows]


def order_matrix():
    out = np.zeros((128, 128), np.float32)
    for row, node in enumerate(node_order()):
        out[row, node] = 1.0
    return out.astype(ml_dtypes.bfloat16)


def moment_tables():
    mu = np.zeros((7, 8))
    for k in range(3):
        mu[k, 4 + k] = 1.0
    mu[3, 0] = 1.0
    for i in (1, 2, 3):
        mu[3 + i, i] = 2.0
        mu[3 + i] -= mu[3 - i]

    def inner(i, j):
        return 0.5 * (mu[i + j] + mu[abs(i - j)])

    tables = np.zeros((3, 4, 8, 8))
    for i in range(4):
        for j in range(4):
            if i + j < 6:
                tables[0, i, :, j] = inner(i, j)
                tables[1, i, :, j] = 0.5 * (inner(i, j + 1) + inner(i, abs(j - 1)))
        tables[2, i, :, 4] = inner(i, 0)
    out = np.zeros((128, 3 * 4 * 128), np.float32)
    for which in range(3):
        for i in range(4):
            start = 128 * (4 * which + i)
            out[:, start : start + 128] = np.kron(tables[which, i], np.eye(16))
    return out.astype(ml_dtypes.bfloat16)


def split(value):
    high = value.astype(BF)
    low = (value - high.astype(F32)).astype(BF)
    return high, low


def dot(left, right):
    return jnp.dot(left, right, preferred_element_type=F32)


def dot_t(left, right):
    return lax.dot_general(left, right, (((1,), (1,)), ((), ())), preferred_element_type=F32)


def exact_dot(value, table):
    rows = value.shape[0]
    high = value.astype(BF)
    rest = value - high.astype(F32)
    middle = rest.astype(BF)
    low = (rest - middle.astype(F32)).astype(BF)
    out = dot(jnp.concatenate([high, middle, low], 0), table)
    return out[0:rows] + out[rows : 2 * rows] + out[2 * rows : 3 * rows]


def iota(shape, axis):
    return lax.broadcasted_iota(jnp.int32, shape, axis)


def ones_where(condition):
    return jnp.where(condition, 1.0, 0.0).astype(BF)


def kernel(
    nx, ny,
    x0_in, lab_in, mat_in, ms_in, kin_in, order_in, table_in,
    xo, ro,
    x0, lab, mat, ms, kin, order, table,
    v, w, rim, corner, ysend, csend, zs, zcs, zr, zcr, tail, zct, kpad, kk, klo, maskb, srow,
    gbuf, fbuf, gm, yst, gres, colr, fhigh, flow,
    es, er, rs, rr, ss, sr, ins,
):
    fetches = [
        pltpu.make_async_copy(src, dst, ins.at[n])
        for n, (src, dst) in enumerate(
            ((x0_in, x0), (kin_in, kin), (order_in, order), (ms_in, ms), (lab_in, lab), (mat_in, mat), (table_in, table))
        )
    ]
    for fetch in fetches:
        fetch.start()

    gx = lax.axis_index("gx")
    gy = lax.axis_index("gy")
    xprev = lax.rem(gx + nx - 1, nx)
    xnext = lax.rem(gx + 1, nx)
    has_prev = gy > 0
    has_next = gy < ny - 1
    yprev = lax.max(gy - 1, 0)
    ynext = lax.min(gy + 1, ny - 1)

    half = ny // 2
    nz = half // 2
    nxx = nx // 4
    y_lo, x_hi = lax.rem(gx, 4), lax.div(gx, 4)
    y_hi, in_half = lax.div(gy, half), lax.rem(gy, half)
    z, core = lax.div(in_half, 2), lax.rem(in_half, 2)
    stages = (
        (0, 8, 4 * y_hi + y_lo, lambda p: (4 * x_hi + lax.rem(p, 4), half * lax.div(p, 4) + in_half)),
        (8, nz, z, lambda p: (gx, half * y_hi + 2 * p + core)),
        (8 + nz, 2 * nxx, 2 * x_hi + core, lambda p: (4 * lax.div(p, 2) + y_lo, half * y_hi + 2 * z + lax.rem(p, 2))),
    )

    barrier = pltpu.get_barrier_semaphore()

    def greet(device):
        pl.semaphore_signal(barrier, inc=1, device_id=device, device_id_type=MESH)

    greet((xprev, gy))
    greet((xnext, gy))

    @pl.when(has_prev)
    def _():
        greet((gx, yprev))
        greet((xprev, yprev))

    @pl.when(has_next)
    def _():
        greet((gx, ynext))
        greet((xnext, ynext))

    for _, size, pos, device in stages:
        def hello(i, carry, size=size, pos=pos, device=device):
            greet(device(lax.rem(pos + i, size)))
            return carry

        lax.fori_loop(1, size, hello, 0)

    kpad[...] = jnp.zeros_like(kpad)
    zct[...] = jnp.zeros_like(zct)
    tail[...] = jnp.zeros_like(tail)
    for fetch in fetches:
        fetch.wait()
    kpad[0:125, 0:125] = kin[...]
    khigh, klow = split(kpad[...])
    pm = order[...]

    def permuted(value):
        return dot_t(dot(pm, value).astype(BF), pm).astype(BF)

    khigh = permuted(khigh)
    kk[:, 0:128] = khigh
    kk[:, 128:256] = khigh
    klo[...] = permuted(klow)
    maskb[...] = jnp.where(lab[...] >= 0, PENALTY, 0.0)
    scale = jnp.zeros((1, 128), F32)
    largest = jnp.zeros((1, 128), F32)
    for which in range(8):
        scale = scale + jnp.where(mat[...] == which, ms[which], 0.0)
        largest = jnp.maximum(largest, jnp.full((1, 128), ms[which], F32))
    srow[...] = jnp.broadcast_to(scale, (8, 128))

    def total(value):
        return jnp.sum(jnp.sum(value, 0, keepdims=True), 1, keepdims=True)

    size = jnp.sqrt(jnp.maximum(total(kpad[...] * kpad[...]), 1e-30))
    unit_k = (kpad[...] / size).astype(BF)
    squared = dot(unit_k, unit_k).astype(BF)
    fourth = dot(squared, squared)
    top = size * jnp.sqrt(jnp.sqrt(jnp.sqrt(total(fourth * fourth))))
    top = PENALTY + largest * top
    colr[0:1, :] = 0.6 * top
    colr[1:2, :] = 0.35 * top
    colr[2:3, :] = 1.0 / (0.35 * top)

    @pl.when(jnp.logical_not(has_next))
    def _():
        rim[:, :, 16:32, :] = jnp.zeros((NQ, CQ, 16, 128), F32)
        corner[...] = jnp.zeros_like(corner)

    @pl.when(jnp.logical_not(has_prev))
    def _():
        zr[:, :, 16:32, :] = jnp.zeros((NQ, CQ, 16, 128), F32)
        zcr[...] = jnp.zeros_like(zcr)

    def rcopy(src, dst, send, recv, device):
        return pltpu.make_async_remote_copy(
            src_ref=src, dst_ref=dst, send_sem=send, recv_sem=recv, device_id=device, device_id_type=MESH
        )

    def ext(src, q):
        first = pl.ds(0, 16)
        return (
            rcopy(src.at[q, :, first], rim.at[q, :, first], es.at[0, q], er.at[0, q], (xprev, gy)),
            rcopy(ysend.at[q], rim.at[q, :, pl.ds(16, 16)], es.at[1, q], er.at[1, q], (gx, yprev)),
            rcopy(csend.at[q], corner.at[q], es.at[2, q], er.at[2, q], (xprev, yprev)),
        )

    def ret(q):
        first, second = pl.ds(0, 16), pl.ds(16, 16)
        return (
            rcopy(zs.at[q, :, first], zr.at[q, :, first], rs.at[0, q], rr.at[0, q], (xnext, gy)),
            rcopy(zs.at[q, :, second], zr.at[q, :, second], rs.at[1, q], rr.at[1, q], (gx, ynext)),
            rcopy(zcs.at[q], zcr.at[q], rs.at[2, q], rr.at[2, q], (xnext, ynext)),
        )

    def extend_start(src, q):
        for j in range(CQ):
            for a in range(4):
                ysend[q, j, 4 * a : 4 * a + 4, :] = src[q, j, 16 * a : 16 * a + 4, :]
            csend[q, 4 * j : 4 * j + 4, :] = src[q, j, 0:4, :]
        copies = ext(src, q)
        copies[0].start()

        @pl.when(has_prev)
        def _():
            copies[1].start()
            copies[2].start()

    def extend_arrived(src, q):
        copies = ext(src, q)
        copies[0].wait_recv()

        @pl.when(has_next)
        def _():
            copies[1].wait_recv()
            copies[2].wait_recv()

    def extend_sent(src, q):
        copies = ext(src, q)
        copies[0].wait_send()

        @pl.when(has_prev)
        def _():
            copies[1].wait_send()
            copies[2].wait_send()

    def return_start(q):
        copies = ret(q)
        copies[0].start()

        @pl.when(has_next)
        def _():
            copies[1].start()
            copies[2].start()

    def return_arrived(q):
        copies = ret(q)
        copies[0].wait_recv()

        @pl.when(has_prev)
        def _():
            copies[1].wait_recv()
            copies[2].wait_recv()

    def return_sent(q):
        copies = ret(q)
        copies[0].wait_send()

        @pl.when(has_next)
        def _():
            copies[1].wait_send()
            copies[2].wait_send()

    def next_plane(value):
        lane = iota(value.shape, 1)
        return jnp.where(lane == 127, 0.0, pltpu.roll(value, 127, 1))

    def prev_plane(value):
        lane = iota(value.shape, 1)
        return jnp.where(lane == 0, 0.0, pltpu.roll(value, 1, 1))

    def cells(src, q):
        blocks = []
        for j in range(CQ):
            tail[q, j, 0:4, :] = corner[q, 4 * j : 4 * j + 4, :]
            tail[q, j, 4:5, :] = next_plane(corner[q, 4 * j : 4 * j + 1, :])
            blocks.append(
                jnp.concatenate(
                    [
                        src[q, j],
                        rim[q, j],
                        next_plane(src[q, j, pl.ds(0, 16, stride=4), :]),
                        next_plane(rim[q, j, pl.ds(0, 8, stride=4), :]),
                        tail[q, j],
                    ],
                    0,
                )
            )
        high, low = split(jnp.concatenate(blocks, 1))
        mapped = dot(kk[...], jnp.concatenate([high, low], 0)) + dot(klo[...], high)
        scales = srow[0:1, :]
        for j in range(CQ):
            out = mapped[:, 128 * j : 128 * j + 128] * scales
            w[q, j] = out[0:64] + maskb[...] * src[q, j]
            w[q, j, pl.ds(0, 16, stride=4), :] += prev_plane(out[96:112])
            zs[q, j] = out[64:96]
            zs[q, j, pl.ds(0, 8, stride=4), :] += prev_plane(out[112:120])
            zct[q, j, 0:4, :] = out[120:124]
            zct[q, j, 0:1, :] += prev_plane(out[124:125])
            zcs[q, 4 * j : 4 * j + 4, :] = zct[q, j, 0:4, :]

    def gather_rims(q):
        for j in range(CQ):
            w[q, j, 0:16, :] += zr[q, j, 0:16, :]
            for a in range(4):
                w[q, j, 16 * a : 16 * a + 4, :] += zr[q, j, 16 + 4 * a : 20 + 4 * a, :]
            w[q, j, 0:4, :] += zcr[q, 4 * j : 4 * j + 4, :]

    def operator(src, number, finish, target):
        def apply(q, carry):
            extend_arrived(src, q)
            if number > 0:
                return_sent(q)
            cells(src, q)
            return_start(q)
            return carry

        lax.fori_loop(0, NQ, apply, 0)
        return functools.partial(_finish, src, number, finish, target)

    def _finish(src, number, finish, target):
        def done(q, carry):
            return_arrived(q)
            extend_sent(src, q)
            gather_rims(q)
            finish(q)
            if number < 4:
                extend_start(target, q)
            return carry

        lax.fori_loop(0, NQ, done, 0)

    def reduce_start(stage, number, buf, value):
        start, size, pos, device = stages[stage]
        buf[start + pos] = value

        def send(i, carry):
            p = lax.rem(pos + i, size)
            here = buf.at[start + pos]
            rcopy(here, here, ss.at[number, start + p], sr.at[number, start + pos], device(p)).start()
            return carry

        lax.fori_loop(1, size, send, 0)

    def reduce_done(stage, number, buf):
        start, size, pos, device = stages[stage]

        def take(i, carry):
            p = lax.rem(pos + i, size)
            here = buf.at[start + p]
            copy = rcopy(here, here, ss.at[number, start + p], sr.at[number, start + p], device(p))
            copy.wait_recv()
            copy.wait_send()
            return carry

        lax.fori_loop(1, size, take, 0)
        total = buf[start]
        for p in range(1, size):
            total = total + buf[start + p]
        return total

    pl.semaphore_wait(
        barrier,
        2 + 7 + (nz - 1) + (2 * nxx - 1) + 2 * (gy > 0).astype(jnp.int32) + 2 * (gy < ny - 1).astype(jnp.int32),
    )

    def first(q, carry):
        extend_start(x0, q)
        return carry

    lax.fori_loop(0, NQ, first, 0)

    def finish0(q):
        for j in range(CQ):
            target = jnp.where(lab[...] == CQ * q + j, 1.0, 0.0)
            v[0, q, j] = target - w[q, j]

    operator(x0, 0, finish0, v.at[0])()

    def finish1(q):
        theta, inverse = colr[0:1, :], colr[2:3, :]
        for j in range(CQ):
            v[1, q, j] = (w[q, j] - theta * v[0, q, j]) * inverse

    operator(v.at[0], 1, finish1, v.at[1])()

    def finish_next(number):
        def finish(q):
            theta, inverse = colr[0:1, :], colr[2:3, :]
            for j in range(CQ):
                v[number, q, j] = 2.0 * (w[q, j] - theta * v[number - 1, q, j]) * inverse - v[number - 2, q, j]

        return finish

    operator(v.at[1], 2, finish_next(2), v.at[2])()

    def grouped(value):
        return [
            value[:, :, 8 * g : 8 * g + 8, :].reshape(8 * COLS, 128) for g in range(value.shape[2] // 8)
        ]

    def stacked(groups):
        high, low = split(jnp.concatenate(groups, 1))
        return jnp.concatenate([high, low], 0)

    def block(left, right):
        out = dot_t(left, right)
        out = out[0:128, 0:128] + out[0:128, 128:256] + out[128:256, 0:128] + out[128:256, 128:256]
        same = (iota((128, 128), 0) & 7) == (iota((128, 128), 1) & 7)
        return jnp.sum(jnp.where(same, out, 0.0).reshape(COLS, 8, 128), 1)

    def placed(value, lane):
        return exact_dot(value, ones_where(iota((128, 128), 1) == lane + (iota((128, 128), 0) >> 3)))

    def grams(number, count, offset):
        yst[...] = stacked(grouped(v[number]))

        def one(j, carry):
            gres[...] += placed(block(stacked(grouped(v[j])), yst[...]), 16 * (offset + j))
            return carry

        lax.fori_loop(0, count, one, 0)

    gres[...] = jnp.zeros_like(gres)
    grams(0, 3, 4)
    operator(v.at[2], 3, finish_next(3), v.at[3])()
    grams(3, 4, 0)
    reduce_start(0, 0, gbuf, gres[...])
    rest = operator(v.at[3], 4, finish_next(4), None)

    last = block(
        stacked(grouped(v[3]) + grouped(rim[...]) + grouped(tail[...])),
        stacked(grouped(w[...]) + grouped(zs[...]) + grouped(zct[...])),
    )
    last = placed(last[0:8], 48) + placed(last[8:16], 64)
    reduce_start(0, 1, fbuf, last)
    reduce_start(1, 0, gbuf, reduce_done(0, 0, gbuf))
    rest()
    reduce_start(1, 1, fbuf, reduce_done(0, 1, fbuf))
    reduce_start(2, 0, gbuf, reduce_done(1, 0, gbuf))
    for j in range(5):
        high, low = split(jnp.concatenate(grouped(v[j]), 1))
        fhigh[128 * j : 128 * j + 128, :] = high
        flow[128 * j : 128 * j + 128, :] = low
    reduce_start(2, 1, fbuf, reduce_done(1, 1, fbuf))

    theta, delta = colr[0:1, :], colr[1:2, :]
    parts = exact_dot(reduce_done(2, 0, gbuf), table[...])
    for i in range(4):
        at = [parts[:, 128 * (4 * which + i) : 128 * (4 * which + i) + 128] for which in range(3)]
        gm[16 * i : 16 * i + 16, :] = theta * at[0] + delta * at[1] + at[2]

    def eliminate(k, carry):
        row = gm[pl.ds(k, 1), :]
        value = gm[...]
        here = iota((64, 128), 1) == k
        col = jnp.sum(jnp.where(here, value, 0.0), 1, keepdims=True)
        pivot = jnp.sum(jnp.where(iota((1, 128), 1) == k, row, 0.0), 1, keepdims=True)
        row = row / pivot
        gm[...] = jnp.where(iota((64, 128), 0) == k, row, value - col * row)
        return carry

    lax.fori_loop(0, 48, eliminate, 0)
    last = reduce_done(2, 1, fbuf)
    inside = (iota((8, 128), 1) >= 48) & (iota((8, 128), 1) < 64)
    gm[48:56, :] += jnp.where(inside, last, 0.0)
    gm[56:64, :] += jnp.where(inside, pltpu.roll(last, 112, 1), 0.0)
    lax.fori_loop(48, 64, eliminate, 0)

    c = [gm[16 * j : 16 * j + 16, :] for j in range(4)]
    half = 0.5 * delta
    unit = jnp.where(iota((16, 128), 0) == iota((16, 128), 1) - 64, 1.0, 0.0)
    e = [
        unit - theta * c[0] - half * c[1],
        -(theta * c[1] + delta * c[0] + half * c[2]),
        -(theta * c[2] + half * (c[1] + c[3])),
        -(theta * c[3] + half * c[2]),
        -(half * c[3]),
    ]
    nothing = jnp.zeros((16, 128), F32)
    forx = jnp.concatenate(c + [nothing] * 4, 0).T
    forr = jnp.concatenate(e + [nothing] * 3, 0).T
    coef = jnp.concatenate([forx[64:80], forr[64:80]], 0)
    spread_in = ones_where((iota((128, 640), 1) >> 3) == iota((128, 640), 0))
    spread_out = ones_where((iota((256, 32), 0) >> 3) == iota((256, 32), 1))
    same = (iota((256, 640), 0) & 7) == (iota((256, 640), 1) & 7)

    def wide(value):
        value = dot(spread_out, dot(value, spread_in).astype(BF))
        return jnp.where(same, value, 0.0).astype(BF)

    chigh, clow = split(coef)
    chigh, clow = wide(chigh), wide(clow)
    for pair in range(4):
        at = slice(256 * pair, 256 * pair + 256)
        high, low = fhigh[:, at], flow[:, at]
        out = dot(chigh, high) + dot(chigh, low) + dot(clow, high)
        for g in (2 * pair, 2 * pair + 1):
            one = out[:, 128 * (g - 2 * pair) : 128 * (g - 2 * pair) + 128]
            xo[:, :, 8 * g : 8 * g + 8, :] = x0[:, :, 8 * g : 8 * g + 8, :] + one[0:128].reshape(NQ, CQ, 8, 128)
            ro[:, :, 8 * g : 8 * g + 8, :] = one[128:256].reshape(NQ, CQ, 8, 128)

    for q in range(NQ):
        return_sent(q)


def on_device(start_block, labels, materials, mat_scales, cell_stiffness):
    nx, ny = lax.axis_size("gx"), lax.axis_size("gy")
    slots = 8 + ny // 4 + nx // 2
    vmem = pl.BlockSpec(memory_space=pltpu.VMEM)
    block = jax.ShapeDtypeStruct((NQ, CQ, 64, 128), F32)
    out = pl.pallas_call(
        functools.partial(kernel, nx, ny),
        out_shape=(block, block),
        in_specs=[pl.BlockSpec(memory_space=pltpu.HBM)] * 7,
        out_specs=(vmem, vmem),
        scratch_shapes=[
            pltpu.VMEM((NQ, CQ, 64, 128), F32),
            pltpu.VMEM((64, 128), jnp.int32),
            pltpu.VMEM((1, 128), jnp.int32),
            pltpu.SMEM((8,), F32),
            pltpu.VMEM((125, 125), F32),
            pltpu.VMEM((128, 128), BF),
            pltpu.VMEM((128, 1536), BF),
            pltpu.VMEM((5, NQ, CQ, 64, 128), F32),
            pltpu.VMEM((NQ, CQ, 64, 128), F32),
            pltpu.VMEM((NQ, CQ, 32, 128), F32),
            pltpu.VMEM((NQ, 4 * CQ, 128), F32),
            pltpu.VMEM((NQ, CQ, 16, 128), F32),
            pltpu.VMEM((NQ, 4 * CQ, 128), F32),
            pltpu.VMEM((NQ, CQ, 32, 128), F32),
            pltpu.VMEM((NQ, 4 * CQ, 128), F32),
            pltpu.VMEM((NQ, CQ, 32, 128), F32),
            pltpu.VMEM((NQ, 4 * CQ, 128), F32),
            pltpu.VMEM((NQ, CQ, 8, 128), F32),
            pltpu.VMEM((NQ, CQ, 8, 128), F32),
            pltpu.VMEM((128, 128), F32),
            pltpu.VMEM((128, 256), BF),
            pltpu.VMEM((128, 128), BF),
            pltpu.VMEM((64, 128), F32),
            pltpu.VMEM((8, 128), F32),
            pltpu.VMEM((slots, 16, 128), F32),
            pltpu.VMEM((slots, 8, 128), F32),
            pltpu.VMEM((64, 128), F32),
            pltpu.VMEM((256, 1024), BF),
            pltpu.VMEM((16, 128), F32),
            pltpu.VMEM((8, 128), F32),
            pltpu.VMEM((640, 1024), BF),
            pltpu.VMEM((640, 1024), BF),
            pltpu.SemaphoreType.DMA((3, NQ)),
            pltpu.SemaphoreType.DMA((3, NQ)),
            pltpu.SemaphoreType.DMA((3, NQ)),
            pltpu.SemaphoreType.DMA((3, NQ)),
            pltpu.SemaphoreType.DMA((2, slots)),
            pltpu.SemaphoreType.DMA((2, slots)),
            pltpu.SemaphoreType.DMA((7,)),
        ],
        compiler_params=pltpu.CompilerParams(
            collective_id=0, has_side_effects=True, vmem_limit_bytes=56 * 1024 * 1024
        ),
    )(
        start_block.reshape(NQ, CQ, 64, 128),
        labels.reshape(64, 128),
        materials.reshape(1, 128),
        mat_scales,
        cell_stiffness,
        jnp.asarray(order_matrix()),
        jnp.asarray(moment_tables()),
    )
    return tuple(one.reshape(start_block.shape) for one in out)


def solution(mesh):
    spread = P(None, "gx", "gy", None, None)
    return jax.shard_map(
        on_device,
        mesh=mesh,
        in_specs=(spread, P("gx", "gy", None, None), P("gx", "gy", None), P(), P()),
        out_specs=(spread, spread),
        check_vma=False,
    )
```

```python
import functools

import jax
import jax.numpy as jnp
import ml_dtypes
import numpy as np
from jax import lax
from jax.experimental import pallas as pl
from jax.experimental.pallas import tpu as pltpu
from jax.sharding import PartitionSpec as P

COLS = 16
NQ = 8
CQ = COLS // NQ
PENALTY = 1.0
MESH = pl.DeviceIdType.MESH
BF = jnp.bfloat16
F32 = jnp.float32


def node_order():
    rows = [(a, b, d) for a in range(4) for b in range(4) for d in range(4)]
    rows += [(4, b, d) for b in range(4) for d in range(4)]
    rows += [(a, 4, d) for a in range(4) for d in range(4)]
    rows += [(a, b, 4) for a in range(4) for b in range(4)]
    rows += [(4, b, 4) for b in range(4)]
    rows += [(a, 4, 4) for a in range(4)]
    rows += [(4, 4, d) for d in range(5)]
    return [25 * a + 5 * b + d for a, b, d in rows]


def order_matrix():
    out = np.zeros((128, 128), np.float32)
    for row, node in enumerate(node_order()):
        out[row, node] = 1.0
    return out.astype(ml_dtypes.bfloat16)


def moment_tables():
    mu = np.zeros((7, 8))
    for k in range(3):
        mu[k, 4 + k] = 1.0
    mu[3, 0] = 1.0
    for i in (1, 2, 3):
        mu[3 + i, i] = 2.0
        mu[3 + i] -= mu[3 - i]

    def inner(i, j):
        return 0.5 * (mu[i + j] + mu[abs(i - j)])

    tables = np.zeros((3, 4, 8, 8))
    for i in range(4):
        for j in range(4):
            if i + j < 6:
                tables[0, i, :, j] = inner(i, j)
                tables[1, i, :, j] = 0.5 * (inner(i, j + 1) + inner(i, abs(j - 1)))
        tables[2, i, :, 4] = inner(i, 0)
    out = np.zeros((128, 3 * 4 * 128), np.float32)
    for which in range(3):
        for i in range(4):
            start = 128 * (4 * which + i)
            out[:, start : start + 128] = np.kron(tables[which, i], np.eye(16))
    return out.astype(ml_dtypes.bfloat16)


def split(value):
    high = value.astype(BF)
    low = (value - high.astype(F32)).astype(BF)
    return high, low


def dot(left, right):
    return jnp.dot(left, right, preferred_element_type=F32)


def dot_t(left, right):
    return lax.dot_general(left, right, (((1,), (1,)), ((), ())), preferred_element_type=F32)


def exact_dot(value, table):
    rows = value.shape[0]
    high = value.astype(BF)
    rest = value - high.astype(F32)
    middle = rest.astype(BF)
    low = (rest - middle.astype(F32)).astype(BF)
    out = dot(jnp.concatenate([high, middle, low], 0), table)
    return out[0:rows] + out[rows : 2 * rows] + out[2 * rows : 3 * rows]


def iota(shape, axis):
    return lax.broadcasted_iota(jnp.int32, shape, axis)


def ones_where(condition):
    return jnp.where(condition, 1.0, 0.0).astype(BF)


def kernel(
    nx, ny,
    x0_in, lab_in, mat_in, ms_in, kin_in, order_in, table_in,
    xo, ro,
    x0, lab, mat, ms, kin, order, table,
    v, w, rim, corner, ysend, csend, zs, zcs, zr, zcr, tail, zct, kpad, kk, klo, maskb, srow,
    gbuf, fbuf, gm, yst, gres, colr, fhigh, flow,
    es, er, rs, rr, ss, sr, ins,
):
    fetches = [
        pltpu.make_async_copy(src, dst, ins.at[n])
        for n, (src, dst) in enumerate(
            ((x0_in, x0), (kin_in, kin), (order_in, order), (ms_in, ms), (lab_in, lab), (mat_in, mat), (table_in, table))
        )
    ]
    for fetch in fetches:
        fetch.start()

    gx = lax.axis_index("gx")
    gy = lax.axis_index("gy")
    xprev = lax.rem(gx + nx - 1, nx)
    xnext = lax.rem(gx + 1, nx)
    has_prev = gy > 0
    has_next = gy < ny - 1
    yprev = lax.max(gy - 1, 0)
    ynext = lax.min(gy + 1, ny - 1)

    half = ny // 2
    nz = half // 2
    nxx = nx // 4
    y_lo, x_hi = lax.rem(gx, 4), lax.div(gx, 4)
    y_hi, in_half = lax.div(gy, half), lax.rem(gy, half)
    z, core = lax.div(in_half, 2), lax.rem(in_half, 2)
    stages = (
        (0, 2 * nxx, 2 * x_hi + core, lambda p: (4 * lax.div(p, 2) + y_lo, half * y_hi + 2 * z + lax.rem(p, 2))),
        (2 * nxx, nz, z, lambda p: (gx, half * y_hi + 2 * p + core)),
        (2 * nxx + nz, 8, 4 * y_hi + y_lo, lambda p: (4 * x_hi + lax.rem(p, 4), half * lax.div(p, 4) + in_half)),
    )

    barrier = pltpu.get_barrier_semaphore()

    def greet(device):
        pl.semaphore_signal(barrier, inc=1, device_id=device, device_id_type=MESH)

    greet((xprev, gy))
    greet((xnext, gy))

    @pl.when(has_prev)
    def _():
        greet((gx, yprev))
        greet((xprev, yprev))

    @pl.when(has_next)
    def _():
        greet((gx, ynext))
        greet((xnext, ynext))

    for _, size, pos, device in stages:
        def hello(i, carry, size=size, pos=pos, device=device):
            greet(device(lax.rem(pos + i, size)))
            return carry

        lax.fori_loop(1, size, hello, 0)

    kpad[...] = jnp.zeros_like(kpad)
    zct[...] = jnp.zeros_like(zct)
    tail[...] = jnp.zeros_like(tail)
    for fetch in fetches:
        fetch.wait()
    kpad[0:125, 0:125] = kin[...]
    khigh, klow = split(kpad[...])
    pm = order[...]

    def permuted(value):
        return dot_t(dot(pm, value).astype(BF), pm).astype(BF)

    khigh = permuted(khigh)
    kk[:, 0:128] = khigh
    kk[:, 128:256] = khigh
    klo[...] = permuted(klow)
    maskb[...] = jnp.where(lab[...] >= 0, PENALTY, 0.0)
    scale = jnp.zeros((1, 128), F32)
    largest = jnp.zeros((1, 128), F32)
    for which in range(8):
        scale = scale + jnp.where(mat[...] == which, ms[which], 0.0)
        largest = jnp.maximum(largest, jnp.full((1, 128), ms[which], F32))
    srow[...] = jnp.broadcast_to(scale, (8, 128))

    def total(value):
        return jnp.sum(jnp.sum(value, 0, keepdims=True), 1, keepdims=True)

    size = jnp.sqrt(jnp.maximum(total(kpad[...] * kpad[...]), 1e-30))
    unit_k = (kpad[...] / size).astype(BF)
    squared = dot(unit_k, unit_k).astype(BF)
    fourth = dot(squared, squared)
    top = size * jnp.sqrt(jnp.sqrt(jnp.sqrt(total(fourth * fourth))))
    top = PENALTY + largest * top
    colr[0:1, :] = 0.6 * top
    colr[1:2, :] = 0.35 * top
    colr[2:3, :] = 1.0 / (0.35 * top)

    @pl.when(jnp.logical_not(has_next))
    def _():
        rim[:, :, 16:32, :] = jnp.zeros((NQ, CQ, 16, 128), F32)
        corner[...] = jnp.zeros_like(corner)

    @pl.when(jnp.logical_not(has_prev))
    def _():
        zr[:, :, 16:32, :] = jnp.zeros((NQ, CQ, 16, 128), F32)
        zcr[...] = jnp.zeros_like(zcr)

    def rcopy(src, dst, send, recv, device):
        return pltpu.make_async_remote_copy(
            src_ref=src, dst_ref=dst, send_sem=send, recv_sem=recv, device_id=device, device_id_type=MESH
        )

    def ext(src, q):
        first = pl.ds(0, 16)
        return (
            rcopy(src.at[q, :, first], rim.at[q, :, first], es.at[0, q], er.at[0, q], (xprev, gy)),
            rcopy(ysend.at[q], rim.at[q, :, pl.ds(16, 16)], es.at[1, q], er.at[1, q], (gx, yprev)),
            rcopy(csend.at[q], corner.at[q], es.at[2, q], er.at[2, q], (xprev, yprev)),
        )

    def ret(q):
        first, second = pl.ds(0, 16), pl.ds(16, 16)
        return (
            rcopy(zs.at[q, :, first], zr.at[q, :, first], rs.at[0, q], rr.at[0, q], (xnext, gy)),
            rcopy(zs.at[q, :, second], zr.at[q, :, second], rs.at[1, q], rr.at[1, q], (gx, ynext)),
            rcopy(zcs.at[q], zcr.at[q], rs.at[2, q], rr.at[2, q], (xnext, ynext)),
        )

    def extend_start(src, q):
        for j in range(CQ):
            for a in range(4):
                ysend[q, j, 4 * a : 4 * a + 4, :] = src[q, j, 16 * a : 16 * a + 4, :]
            csend[q, 4 * j : 4 * j + 4, :] = src[q, j, 0:4, :]
        copies = ext(src, q)

        @pl.when(has_prev)
        def _():
            copies[2].start()
            copies[1].start()

        copies[0].start()

    def extend_arrived(src, q):
        copies = ext(src, q)
        copies[0].wait_recv()

        @pl.when(has_next)
        def _():
            copies[1].wait_recv()
            copies[2].wait_recv()

    def extend_sent(src, q):
        copies = ext(src, q)
        copies[0].wait_send()

        @pl.when(has_prev)
        def _():
            copies[1].wait_send()
            copies[2].wait_send()

    def return_start(q):
        copies = ret(q)

        @pl.when(has_next)
        def _():
            copies[2].start()
            copies[1].start()

        copies[0].start()

    def return_arrived(q):
        copies = ret(q)
        copies[0].wait_recv()

        @pl.when(has_prev)
        def _():
            copies[1].wait_recv()
            copies[2].wait_recv()

    def return_sent(q):
        copies = ret(q)
        copies[0].wait_send()

        @pl.when(has_next)
        def _():
            copies[1].wait_send()
            copies[2].wait_send()

    def next_plane(value):
        lane = iota(value.shape, 1)
        return jnp.where(lane == 127, 0.0, pltpu.roll(value, 127, 1))

    def prev_plane(value):
        lane = iota(value.shape, 1)
        return jnp.where(lane == 0, 0.0, pltpu.roll(value, 1, 1))

    def cells(src, q):
        blocks = []
        for j in range(CQ):
            tail[q, j, 0:4, :] = corner[q, 4 * j : 4 * j + 4, :]
            tail[q, j, 4:5, :] = next_plane(corner[q, 4 * j : 4 * j + 1, :])
            blocks.append(
                jnp.concatenate(
                    [
                        src[q, j],
                        rim[q, j],
                        next_plane(src[q, j, pl.ds(0, 16, stride=4), :]),
                        next_plane(rim[q, j, pl.ds(0, 8, stride=4), :]),
                        tail[q, j],
                    ],
                    0,
                )
            )
        high, low = split(jnp.concatenate(blocks, 1))
        mapped = dot(kk[...], jnp.concatenate([high, low], 0)) + dot(klo[...], high)
        scales = srow[0:1, :]
        for j in range(CQ):
            out = mapped[:, 128 * j : 128 * j + 128] * scales
            w[q, j] = out[0:64] + maskb[...] * src[q, j]
            w[q, j, pl.ds(0, 16, stride=4), :] += prev_plane(out[96:112])
            zs[q, j] = out[64:96]
            zs[q, j, pl.ds(0, 8, stride=4), :] += prev_plane(out[112:120])
            zct[q, j, 0:4, :] = out[120:124]
            zct[q, j, 0:1, :] += prev_plane(out[124:125])
            zcs[q, 4 * j : 4 * j + 4, :] = zct[q, j, 0:4, :]

    def gather_rims(q):
        for j in range(CQ):
            w[q, j, 0:16, :] += zr[q, j, 0:16, :]
            for a in range(4):
                w[q, j, 16 * a : 16 * a + 4, :] += zr[q, j, 16 + 4 * a : 20 + 4 * a, :]
            w[q, j, 0:4, :] += zcr[q, 4 * j : 4 * j + 4, :]

    def operator(src, number, finish, target):
        def apply(q, carry):
            extend_arrived(src, q)
            if number > 0:
                return_sent(q)
            cells(src, q)
            return_start(q)
            return carry

        lax.fori_loop(0, NQ, apply, 0)
        return functools.partial(_finish, src, number, finish, target)

    def operate(src, number, finish, target):
        lag = NQ - 2

        def apply(q):
            extend_arrived(src, q)
            if number > 0:
                return_sent(q)
            cells(src, q)
            return_start(q)

        def done(q):
            return_arrived(q)
            extend_sent(src, q)
            gather_rims(q)
            finish(q)
            extend_start(target, q)

        def lead(q, carry):
            apply(q)
            return carry

        def both(q, carry):
            apply(q)
            done(q - lag)
            return carry

        def trail(q, carry):
            done(q)
            return carry

        lax.fori_loop(0, lag, lead, 0)
        lax.fori_loop(lag, NQ, both, 0)
        lax.fori_loop(NQ - lag, NQ, trail, 0)

    def _finish(src, number, finish, target):
        def done(q, carry):
            return_arrived(q)
            extend_sent(src, q)
            gather_rims(q)
            finish(q)
            if number < 4:
                extend_start(target, q)
            return carry

        lax.fori_loop(0, NQ, done, 0)

    def reduce_start(stage, number, buf, value):
        start, size, pos, device = stages[stage]
        buf[start + pos] = value

        def send(i, carry):
            p = lax.rem(pos + i, size)
            here = buf.at[start + pos]
            rcopy(here, here, ss.at[number, start + p], sr.at[number, start + pos], device(p)).start()
            return carry

        lax.fori_loop(1, size, send, 0)

    def reduce_done(stage, number, buf):
        start, size, pos, device = stages[stage]

        def take(i, carry):
            p = lax.rem(pos + i, size)
            here = buf.at[start + p]
            copy = rcopy(here, here, ss.at[number, start + p], sr.at[number, start + p], device(p))
            copy.wait_recv()
            copy.wait_send()
            return carry

        lax.fori_loop(1, size, take, 0)
        total = buf[start]
        for p in range(1, size):
            total = total + buf[start + p]
        return total

    pl.semaphore_wait(
        barrier,
        2 + 7 + (nz - 1) + (2 * nxx - 1) + 2 * (gy > 0).astype(jnp.int32) + 2 * (gy < ny - 1).astype(jnp.int32),
    )

    def first(q, carry):
        extend_start(x0, q)
        return carry

    lax.fori_loop(0, NQ, first, 0)

    def finish0(q):
        for j in range(CQ):
            target = jnp.where(lab[...] == CQ * q + j, 1.0, 0.0)
            v[0, q, j] = target - w[q, j]

    operate(x0, 0, finish0, v.at[0])

    def finish1(q):
        theta, inverse = colr[0:1, :], colr[2:3, :]
        for j in range(CQ):
            v[1, q, j] = (w[q, j] - theta * v[0, q, j]) * inverse

    operate(v.at[0], 1, finish1, v.at[1])

    def finish_next(number):
        def finish(q):
            theta, inverse = colr[0:1, :], colr[2:3, :]
            for j in range(CQ):
                v[number, q, j] = 2.0 * (w[q, j] - theta * v[number - 1, q, j]) * inverse - v[number - 2, q, j]

        return finish

    operate(v.at[1], 2, finish_next(2), v.at[2])

    def grouped(value):
        return [
            value[:, :, 8 * g : 8 * g + 8, :].reshape(8 * COLS, 128) for g in range(value.shape[2] // 8)
        ]

    def stacked(groups):
        high, low = split(jnp.concatenate(groups, 1))
        return jnp.concatenate([high, low], 0)

    def block(left, right):
        out = dot_t(left, right)
        out = out[0:128, 0:128] + out[0:128, 128:256] + out[128:256, 0:128] + out[128:256, 128:256]
        same = (iota((128, 128), 0) & 7) == (iota((128, 128), 1) & 7)
        return jnp.sum(jnp.where(same, out, 0.0).reshape(COLS, 8, 128), 1)

    def placed(value, lane):
        return exact_dot(value, ones_where(iota((128, 128), 1) == lane + (iota((128, 128), 0) >> 3)))

    def grams(number, count, offset):
        yst[...] = stacked(grouped(v[number]))

        def one(j, carry):
            gres[...] += placed(block(stacked(grouped(v[j])), yst[...]), 16 * (offset + j))
            return carry

        lax.fori_loop(0, count, one, 0)

    gres[...] = jnp.zeros_like(gres)
    grams(0, 3, 4)
    operate(v.at[2], 3, finish_next(3), v.at[3])
    grams(3, 4, 0)
    reduce_start(0, 0, gbuf, gres[...])
    rest = operator(v.at[3], 4, finish_next(4), None)

    last = block(
        stacked(grouped(v[3]) + grouped(rim[...]) + grouped(tail[...])),
        stacked(grouped(w[...]) + grouped(zs[...]) + grouped(zct[...])),
    )
    last = placed(last[0:8], 48) + placed(last[8:16], 64)
    reduce_start(0, 1, fbuf, last)
    reduce_start(1, 0, gbuf, reduce_done(0, 0, gbuf))
    reduce_start(1, 1, fbuf, reduce_done(0, 1, fbuf))
    reduce_start(2, 0, gbuf, reduce_done(1, 0, gbuf))
    rest()
    for j in range(5):
        high, low = split(jnp.concatenate(grouped(v[j]), 1))
        fhigh[128 * j : 128 * j + 128, :] = high
        flow[128 * j : 128 * j + 128, :] = low
    reduce_start(2, 1, fbuf, reduce_done(1, 1, fbuf))

    theta, delta = colr[0:1, :], colr[1:2, :]
    parts = exact_dot(reduce_done(2, 0, gbuf), table[...])
    for i in range(4):
        at = [parts[:, 128 * (4 * which + i) : 128 * (4 * which + i) + 128] for which in range(3)]
        gm[16 * i : 16 * i + 16, :] = theta * at[0] + delta * at[1] + at[2]

    def eliminate(k, carry):
        row = gm[pl.ds(k, 1), :]
        value = gm[...]
        here = iota((64, 128), 1) == k
        col = jnp.sum(jnp.where(here, value, 0.0), 1, keepdims=True)
        pivot = jnp.sum(jnp.where(iota((1, 128), 1) == k, row, 0.0), 1, keepdims=True)
        row = row / pivot
        gm[...] = jnp.where(iota((64, 128), 0) == k, row, value - col * row)
        return carry

    lax.fori_loop(0, 48, eliminate, 0)
    last = reduce_done(2, 1, fbuf)
    inside = (iota((8, 128), 1) >= 48) & (iota((8, 128), 1) < 64)
    gm[48:56, :] += jnp.where(inside, last, 0.0)
    gm[56:64, :] += jnp.where(inside, pltpu.roll(last, 112, 1), 0.0)
    lax.fori_loop(48, 64, eliminate, 0)

    c = [gm[16 * j : 16 * j + 16, :] for j in range(4)]
    half = 0.5 * delta
    unit = jnp.where(iota((16, 128), 0) == iota((16, 128), 1) - 64, 1.0, 0.0)
    e = [
        unit - theta * c[0] - half * c[1],
        -(theta * c[1] + delta * c[0] + half * c[2]),
        -(theta * c[2] + half * (c[1] + c[3])),
        -(theta * c[3] + half * c[2]),
        -(half * c[3]),
    ]
    nothing = jnp.zeros((16, 128), F32)
    forx = jnp.concatenate(c + [nothing] * 4, 0).T
    forr = jnp.concatenate(e + [nothing] * 3, 0).T
    coef = jnp.concatenate([forx[64:80], forr[64:80]], 0)
    spread_in = ones_where((iota((128, 640), 1) >> 3) == iota((128, 640), 0))
    spread_out = ones_where((iota((256, 32), 0) >> 3) == iota((256, 32), 1))
    same = (iota((256, 640), 0) & 7) == (iota((256, 640), 1) & 7)

    def wide(value):
        value = dot(spread_out, dot(value, spread_in).astype(BF))
        return jnp.where(same, value, 0.0).astype(BF)

    chigh, clow = split(coef)
    chigh, clow = wide(chigh), wide(clow)
    for pair in range(4):
        at = slice(256 * pair, 256 * pair + 256)
        high, low = fhigh[:, at], flow[:, at]
        out = dot(chigh, high) + dot(chigh, low) + dot(clow, high)
        for g in (2 * pair, 2 * pair + 1):
            one = out[:, 128 * (g - 2 * pair) : 128 * (g - 2 * pair) + 128]
            xo[:, :, 8 * g : 8 * g + 8, :] = x0[:, :, 8 * g : 8 * g + 8, :] + one[0:128].reshape(NQ, CQ, 8, 128)
            ro[:, :, 8 * g : 8 * g + 8, :] = one[128:256].reshape(NQ, CQ, 8, 128)

    for q in range(NQ):
        return_sent(q)


def on_device(start_block, labels, materials, mat_scales, cell_stiffness):
    nx, ny = lax.axis_size("gx"), lax.axis_size("gy")
    slots = 8 + ny // 4 + nx // 2
    vmem = pl.BlockSpec(memory_space=pltpu.VMEM)
    block = jax.ShapeDtypeStruct((NQ, CQ, 64, 128), F32)
    out = pl.pallas_call(
        functools.partial(kernel, nx, ny),
        out_shape=(block, block),
        in_specs=[pl.BlockSpec(memory_space=pltpu.HBM)] * 7,
        out_specs=(vmem, vmem),
        scratch_shapes=[
            pltpu.VMEM((NQ, CQ, 64, 128), F32),
            pltpu.VMEM((64, 128), jnp.int32),
            pltpu.VMEM((1, 128), jnp.int32),
            pltpu.SMEM((8,), F32),
            pltpu.VMEM((125, 125), F32),
            pltpu.VMEM((128, 128), BF),
            pltpu.VMEM((128, 1536), BF),
            pltpu.VMEM((5, NQ, CQ, 64, 128), F32),
            pltpu.VMEM((NQ, CQ, 64, 128), F32),
            pltpu.VMEM((NQ, CQ, 32, 128), F32),
            pltpu.VMEM((NQ, 4 * CQ, 128), F32),
            pltpu.VMEM((NQ, CQ, 16, 128), F32),
            pltpu.VMEM((NQ, 4 * CQ, 128), F32),
            pltpu.VMEM((NQ, CQ, 32, 128), F32),
            pltpu.VMEM((NQ, 4 * CQ, 128), F32),
            pltpu.VMEM((NQ, CQ, 32, 128), F32),
            pltpu.VMEM((NQ, 4 * CQ, 128), F32),
            pltpu.VMEM((NQ, CQ, 8, 128), F32),
            pltpu.VMEM((NQ, CQ, 8, 128), F32),
            pltpu.VMEM((128, 128), F32),
            pltpu.VMEM((128, 256), BF),
            pltpu.VMEM((128, 128), BF),
            pltpu.VMEM((64, 128), F32),
            pltpu.VMEM((8, 128), F32),
            pltpu.VMEM((slots, 16, 128), F32),
            pltpu.VMEM((slots, 8, 128), F32),
            pltpu.VMEM((64, 128), F32),
            pltpu.VMEM((256, 1024), BF),
            pltpu.VMEM((16, 128), F32),
            pltpu.VMEM((8, 128), F32),
            pltpu.VMEM((640, 1024), BF),
            pltpu.VMEM((640, 1024), BF),
            pltpu.SemaphoreType.DMA((3, NQ)),
            pltpu.SemaphoreType.DMA((3, NQ)),
            pltpu.SemaphoreType.DMA((3, NQ)),
            pltpu.SemaphoreType.DMA((3, NQ)),
            pltpu.SemaphoreType.DMA((2, slots)),
            pltpu.SemaphoreType.DMA((2, slots)),
            pltpu.SemaphoreType.DMA((7,)),
        ],
        compiler_params=pltpu.CompilerParams(
            collective_id=0, has_side_effects=True, vmem_limit_bytes=56 * 1024 * 1024
        ),
    )(
        start_block.reshape(NQ, CQ, 64, 128),
        labels.reshape(64, 128),
        materials.reshape(1, 128),
        mat_scales,
        cell_stiffness,
        jnp.asarray(order_matrix()),
        jnp.asarray(moment_tables()),
    )
    return tuple(one.reshape(start_block.shape) for one in out)


def solution(mesh):
    spread = P(None, "gx", "gy", None, None)
    return jax.shard_map(
        on_device,
        mesh=mesh,
        in_specs=(spread, P("gx", "gy", None, None), P("gx", "gy", None), P(), P()),
        out_specs=(spread, spread),
        check_vma=False,
    )
```

```python
import functools

import jax
import jax.numpy as jnp
import ml_dtypes
import numpy as np
from jax import lax
from jax.experimental import pallas as pl
from jax.experimental.pallas import tpu as pltpu
from jax.sharding import PartitionSpec as P

COLS = 16
NQ = 8
CQ = COLS // NQ
PENALTY = 1.0
MESH = pl.DeviceIdType.MESH
BF = jnp.bfloat16
F32 = jnp.float32


def node_order():
    rows = [(a, b, d) for a in range(4) for b in range(4) for d in range(4)]
    rows += [(4, b, d) for b in range(4) for d in range(4)]
    rows += [(a, 4, d) for a in range(4) for d in range(4)]
    rows += [(a, b, 4) for a in range(4) for b in range(4)]
    rows += [(4, b, 4) for b in range(4)]
    rows += [(a, 4, 4) for a in range(4)]
    rows += [(4, 4, d) for d in range(5)]
    return [25 * a + 5 * b + d for a, b, d in rows]


def order_matrix():
    out = np.zeros((128, 128), np.float32)
    for row, node in enumerate(node_order()):
        out[row, node] = 1.0
    return out.astype(ml_dtypes.bfloat16)


def moment_tables():
    mu = np.zeros((7, 8))
    for k in range(3):
        mu[k, 4 + k] = 1.0
    mu[3, 0] = 1.0
    for i in (1, 2, 3):
        mu[3 + i, i] = 2.0
        mu[3 + i] -= mu[3 - i]

    def inner(i, j):
        return 0.5 * (mu[i + j] + mu[abs(i - j)])

    tables = np.zeros((3, 4, 8, 8))
    for i in range(4):
        for j in range(4):
            if i + j < 6:
                tables[0, i, :, j] = inner(i, j)
                tables[1, i, :, j] = 0.5 * (inner(i, j + 1) + inner(i, abs(j - 1)))
        tables[2, i, :, 4] = inner(i, 0)
    out = np.zeros((128, 3 * 4 * 128), np.float32)
    for which in range(3):
        for i in range(4):
            start = 128 * (4 * which + i)
            out[:, start : start + 128] = np.kron(tables[which, i], np.eye(16))
    return out.astype(ml_dtypes.bfloat16)


def split(value):
    high = value.astype(BF)
    low = (value - high.astype(F32)).astype(BF)
    return high, low


def dot(left, right):
    return jnp.dot(left, right, preferred_element_type=F32)


def dot_t(left, right):
    return lax.dot_general(left, right, (((1,), (1,)), ((), ())), preferred_element_type=F32)


def exact_dot(value, table):
    rows = value.shape[0]
    high = value.astype(BF)
    rest = value - high.astype(F32)
    middle = rest.astype(BF)
    low = (rest - middle.astype(F32)).astype(BF)
    out = dot(jnp.concatenate([high, middle, low], 0), table)
    return out[0:rows] + out[rows : 2 * rows] + out[2 * rows : 3 * rows]


def iota(shape, axis):
    return lax.broadcasted_iota(jnp.int32, shape, axis)


def ones_where(condition):
    return jnp.where(condition, 1.0, 0.0).astype(BF)


def kernel(
    nx, ny,
    x0_in, lab_in, mat_in, ms_in, kin_in, order_in, table_in,
    xo_out, ro_out,
    xo, ro, x0, lab, mat, ms, kin, order, table,
    v, w, rim, corner, ysend, csend, zs, zcs, zr, zcr, tail, zct, kpad, kk, klo, maskb, srow,
    gbuf, fbuf, gm, yst, gres, colr, fhigh, flow,
    es, er, rs, rr, ss, sr, ins, outs,
):
    fetches = [
        pltpu.make_async_copy(src, dst, ins.at[n])
        for n, (src, dst) in enumerate(
            ((x0_in, x0), (kin_in, kin), (order_in, order), (ms_in, ms), (lab_in, lab), (mat_in, mat), (table_in, table))
        )
    ]
    for fetch in fetches:
        fetch.start()

    gx = lax.axis_index("gx")
    gy = lax.axis_index("gy")
    xprev = lax.rem(gx + nx - 1, nx)
    xnext = lax.rem(gx + 1, nx)
    has_prev = gy > 0
    has_next = gy < ny - 1
    yprev = lax.max(gy - 1, 0)
    ynext = lax.min(gy + 1, ny - 1)

    half = ny // 2
    nz = half // 2
    nxx = nx // 4
    y_lo, x_hi = lax.rem(gx, 4), lax.div(gx, 4)
    y_hi, in_half = lax.div(gy, half), lax.rem(gy, half)
    z, core = lax.div(in_half, 2), lax.rem(in_half, 2)
    stages = (
        (0, 2 * nxx, 2 * x_hi + core, lambda p: (4 * lax.div(p, 2) + y_lo, half * y_hi + 2 * z + lax.rem(p, 2))),
        (2 * nxx, nz, z, lambda p: (gx, half * y_hi + 2 * p + core)),
        (2 * nxx + nz, 8, 4 * y_hi + y_lo, lambda p: (4 * x_hi + lax.rem(p, 4), half * lax.div(p, 4) + in_half)),
    )

    barrier = pltpu.get_barrier_semaphore()

    def greet(device):
        pl.semaphore_signal(barrier, inc=1, device_id=device, device_id_type=MESH)

    greet((xprev, gy))
    greet((xnext, gy))

    @pl.when(has_prev)
    def _():
        greet((gx, yprev))
        greet((xprev, yprev))

    @pl.when(has_next)
    def _():
        greet((gx, ynext))
        greet((xnext, ynext))

    for _, size, pos, device in stages:
        def hello(i, carry, size=size, pos=pos, device=device):
            greet(device(lax.rem(pos + i, size)))
            return carry

        lax.fori_loop(1, size, hello, 0)

    kpad[...] = jnp.zeros_like(kpad)
    zct[...] = jnp.zeros_like(zct)
    tail[...] = jnp.zeros_like(tail)
    for fetch in fetches:
        fetch.wait()
    kpad[0:125, 0:125] = kin[...]
    khigh, klow = split(kpad[...])
    pm = order[...]

    def permuted(value):
        return dot_t(dot(pm, value).astype(BF), pm).astype(BF)

    khigh = permuted(khigh)
    kk[:, 0:128] = khigh
    kk[:, 128:256] = khigh
    klo[...] = permuted(klow)
    maskb[...] = jnp.where(lab[...] >= 0, PENALTY, 0.0)
    scale = jnp.zeros((1, 128), F32)
    largest = jnp.zeros((1, 128), F32)
    for which in range(8):
        scale = scale + jnp.where(mat[...] == which, ms[which], 0.0)
        largest = jnp.maximum(largest, jnp.full((1, 128), ms[which], F32))
    srow[...] = jnp.broadcast_to(scale, (8, 128))

    def total(value):
        return jnp.sum(jnp.sum(value, 0, keepdims=True), 1, keepdims=True)

    size = jnp.sqrt(jnp.maximum(total(kpad[...] * kpad[...]), 1e-30))
    unit_k = (kpad[...] / size).astype(BF)
    squared = dot(unit_k, unit_k).astype(BF)
    fourth = dot(squared, squared)
    top = size * jnp.sqrt(jnp.sqrt(jnp.sqrt(total(fourth * fourth))))
    top = PENALTY + largest * top
    colr[0:1, :] = 0.6 * top
    colr[1:2, :] = 0.35 * top
    colr[2:3, :] = 1.0 / (0.35 * top)

    @pl.when(jnp.logical_not(has_next))
    def _():
        rim[:, :, 16:32, :] = jnp.zeros((NQ, CQ, 16, 128), F32)
        corner[...] = jnp.zeros_like(corner)

    @pl.when(jnp.logical_not(has_prev))
    def _():
        zr[:, :, 16:32, :] = jnp.zeros((NQ, CQ, 16, 128), F32)
        zcr[...] = jnp.zeros_like(zcr)

    def rcopy(src, dst, send, recv, device):
        return pltpu.make_async_remote_copy(
            src_ref=src, dst_ref=dst, send_sem=send, recv_sem=recv, device_id=device, device_id_type=MESH
        )

    def ext(src, q):
        first = pl.ds(0, 16)
        return (
            rcopy(src.at[q, :, first], rim.at[q, :, first], es.at[0, q], er.at[0, q], (xprev, gy)),
            rcopy(ysend.at[q], rim.at[q, :, pl.ds(16, 16)], es.at[1, q], er.at[1, q], (gx, yprev)),
            rcopy(csend.at[q], corner.at[q], es.at[2, q], er.at[2, q], (xprev, yprev)),
        )

    def ret(q):
        first, second = pl.ds(0, 16), pl.ds(16, 16)
        return (
            rcopy(zs.at[q, :, first], zr.at[q, :, first], rs.at[0, q], rr.at[0, q], (xnext, gy)),
            rcopy(zs.at[q, :, second], zr.at[q, :, second], rs.at[1, q], rr.at[1, q], (gx, ynext)),
            rcopy(zcs.at[q], zcr.at[q], rs.at[2, q], rr.at[2, q], (xnext, ynext)),
        )

    def extend_start(src, q):
        for j in range(CQ):
            for a in range(4):
                ysend[q, j, 4 * a : 4 * a + 4, :] = src[q, j, 16 * a : 16 * a + 4, :]
            csend[q, 4 * j : 4 * j + 4, :] = src[q, j, 0:4, :]
        copies = ext(src, q)

        @pl.when(has_prev)
        def _():
            copies[2].start()
            copies[1].start()

        copies[0].start()

    def extend_arrived(src, q):
        copies = ext(src, q)
        copies[0].wait_recv()

        @pl.when(has_next)
        def _():
            copies[1].wait_recv()
            copies[2].wait_recv()

    def extend_sent(src, q):
        copies = ext(src, q)
        copies[0].wait_send()

        @pl.when(has_prev)
        def _():
            copies[1].wait_send()
            copies[2].wait_send()

    def return_start(q):
        copies = ret(q)

        @pl.when(has_next)
        def _():
            copies[2].start()
            copies[1].start()

        copies[0].start()

    def return_arrived(q):
        copies = ret(q)
        copies[0].wait_recv()

        @pl.when(has_prev)
        def _():
            copies[1].wait_recv()
            copies[2].wait_recv()

    def return_sent(q):
        copies = ret(q)
        copies[0].wait_send()

        @pl.when(has_next)
        def _():
            copies[1].wait_send()
            copies[2].wait_send()

    def next_plane(value):
        lane = iota(value.shape, 1)
        return jnp.where(lane == 127, 0.0, pltpu.roll(value, 127, 1))

    def prev_plane(value):
        lane = iota(value.shape, 1)
        return jnp.where(lane == 0, 0.0, pltpu.roll(value, 1, 1))

    def cells(src, q):
        blocks = []
        for j in range(CQ):
            tail[q, j, 0:4, :] = corner[q, 4 * j : 4 * j + 4, :]
            tail[q, j, 4:5, :] = next_plane(corner[q, 4 * j : 4 * j + 1, :])
            blocks.append(
                jnp.concatenate(
                    [
                        src[q, j],
                        rim[q, j],
                        next_plane(src[q, j, pl.ds(0, 16, stride=4), :]),
                        next_plane(rim[q, j, pl.ds(0, 8, stride=4), :]),
                        tail[q, j],
                    ],
                    0,
                )
            )
        high, low = split(jnp.concatenate(blocks, 1))
        mapped = dot(kk[...], jnp.concatenate([high, low], 0)) + dot(klo[...], high)
        scales = srow[0:1, :]
        for j in range(CQ):
            out = mapped[:, 128 * j : 128 * j + 128] * scales
            w[q, j] = out[0:64] + maskb[...] * src[q, j]
            w[q, j, pl.ds(0, 16, stride=4), :] += prev_plane(out[96:112])
            zs[q, j] = out[64:96]
            zs[q, j, pl.ds(0, 8, stride=4), :] += prev_plane(out[112:120])
            zct[q, j, 0:4, :] = out[120:124]
            zct[q, j, 0:1, :] += prev_plane(out[124:125])
            zcs[q, 4 * j : 4 * j + 4, :] = zct[q, j, 0:4, :]

    def gather_rims(q):
        for j in range(CQ):
            w[q, j, 0:16, :] += zr[q, j, 0:16, :]
            for a in range(4):
                w[q, j, 16 * a : 16 * a + 4, :] += zr[q, j, 16 + 4 * a : 20 + 4 * a, :]
            w[q, j, 0:4, :] += zcr[q, 4 * j : 4 * j + 4, :]

    def operate(src, number, finish, target, between=None, after=None):
        lag = NQ - 4

        def apply(q):
            extend_arrived(src, q)
            if number > 0:
                return_sent(q)
            cells(src, q)
            return_start(q)

        def done(q):
            return_arrived(q)
            extend_sent(src, q)
            gather_rims(q)
            finish(q)
            if target is not None:
                extend_start(target, q)

        def lead(q, carry):
            apply(q)
            return carry

        def both(q, carry):
            apply(q)
            done(q - lag)
            return carry

        def trail(q, carry):
            done(q)
            return carry

        lax.fori_loop(0, lag, lead, 0)
        if between is None:
            lax.fori_loop(lag, NQ, both, 0)
            lax.fori_loop(NQ - lag, NQ, trail, 0)
        else:
            between()
            lax.fori_loop(lag, NQ, lead, 0)
            after()
            lax.fori_loop(0, NQ, trail, 0)

    def reduce_start(stage, number, buf, value):
        start, size, pos, device = stages[stage]
        buf[start + pos] = value

        def send(i, carry):
            p = lax.rem(pos + i, size)
            here = buf.at[start + pos]
            rcopy(here, here, ss.at[number, start + p], sr.at[number, start + pos], device(p)).start()
            return carry

        lax.fori_loop(1, size, send, 0)

    def reduce_done(stage, number, buf):
        start, size, pos, device = stages[stage]

        def take(i, carry):
            p = lax.rem(pos + i, size)
            here = buf.at[start + p]
            copy = rcopy(here, here, ss.at[number, start + p], sr.at[number, start + p], device(p))
            copy.wait_recv()
            copy.wait_send()
            return carry

        lax.fori_loop(1, size, take, 0)
        total = buf[start]
        for p in range(1, size):
            total = total + buf[start + p]
        return total

    pl.semaphore_wait(
        barrier,
        2 + 7 + (nz - 1) + (2 * nxx - 1) + 2 * (gy > 0).astype(jnp.int32) + 2 * (gy < ny - 1).astype(jnp.int32),
    )

    def first(q, carry):
        extend_start(x0, q)
        return carry

    lax.fori_loop(0, NQ, first, 0)

    def finish0(q):
        for j in range(CQ):
            target = jnp.where(lab[...] == CQ * q + j, 1.0, 0.0)
            v[0, q, j] = target - w[q, j]

    operate(x0, 0, finish0, v.at[0])

    def finish1(q):
        theta, inverse = colr[0:1, :], colr[2:3, :]
        for j in range(CQ):
            v[1, q, j] = (w[q, j] - theta * v[0, q, j]) * inverse

    operate(v.at[0], 1, finish1, v.at[1])

    def finish_next(number):
        def finish(q):
            theta, inverse = colr[0:1, :], colr[2:3, :]
            for j in range(CQ):
                v[number, q, j] = 2.0 * (w[q, j] - theta * v[number - 1, q, j]) * inverse - v[number - 2, q, j]

        return finish

    operate(v.at[1], 2, finish_next(2), v.at[2])

    def grouped(value):
        return [
            value[:, :, 8 * g : 8 * g + 8, :].reshape(8 * COLS, 128) for g in range(value.shape[2] // 8)
        ]

    def stacked(groups):
        high, low = split(jnp.concatenate(groups, 1))
        return jnp.concatenate([high, low], 0)

    def block(left, right):
        out = dot_t(left, right)
        out = out[0:128, 0:128] + out[0:128, 128:256] + out[128:256, 0:128] + out[128:256, 128:256]
        same = (iota((128, 128), 0) & 7) == (iota((128, 128), 1) & 7)
        return jnp.sum(jnp.where(same, out, 0.0).reshape(COLS, 8, 128), 1)

    def placed(value, lane):
        return exact_dot(value, ones_where(iota((128, 128), 1) == lane + (iota((128, 128), 0) >> 3)))

    def grams(number, count, offset):
        yst[...] = stacked(grouped(v[number]))

        def one(j, carry):
            gres[...] += placed(block(stacked(grouped(v[j])), yst[...]), 16 * (offset + j))
            return carry

        lax.fori_loop(0, count, one, 0)

    gres[...] = jnp.zeros_like(gres)
    grams(0, 3, 4)
    operate(v.at[2], 3, finish_next(3), v.at[3])
    grams(3, 4, 0)
    reduce_start(0, 0, gbuf, gres[...])

    def between():
        reduce_start(1, 0, gbuf, reduce_done(0, 0, gbuf))

    def after():
        last = block(
            stacked(grouped(v[3]) + grouped(rim[...]) + grouped(tail[...])),
            stacked(grouped(w[...]) + grouped(zs[...]) + grouped(zct[...])),
        )
        reduce_start(0, 1, fbuf, placed(last[0:8], 48) + placed(last[8:16], 64))
        reduce_start(2, 0, gbuf, reduce_done(1, 0, gbuf))
        reduce_start(1, 1, fbuf, reduce_done(0, 1, fbuf))

    operate(v.at[3], 4, finish_next(4), None, between, after)

    theta, delta = colr[0:1, :], colr[1:2, :]
    parts = exact_dot(reduce_done(2, 0, gbuf), table[...])
    for i in range(4):
        at = [parts[:, 128 * (4 * which + i) : 128 * (4 * which + i) + 128] for which in range(3)]
        gm[16 * i : 16 * i + 16, :] = theta * at[0] + delta * at[1] + at[2]

    def eliminate(k, carry):
        row = gm[pl.ds(k, 1), :]
        value = gm[...]
        here = iota((64, 128), 1) == k
        col = jnp.sum(jnp.where(here, value, 0.0), 1, keepdims=True)
        pivot = jnp.sum(jnp.where(iota((1, 128), 1) == k, row, 0.0), 1, keepdims=True)
        row = row / pivot
        gm[...] = jnp.where(iota((64, 128), 0) == k, row, value - col * row)
        return carry

    lax.fori_loop(0, 16, eliminate, 0)
    reduce_start(2, 1, fbuf, reduce_done(1, 1, fbuf))
    lax.fori_loop(16, 48, eliminate, 0)
    for j in range(5):
        high, low = split(jnp.concatenate(grouped(v[j]), 1))
        fhigh[128 * j : 128 * j + 128, :] = high
        flow[128 * j : 128 * j + 128, :] = low
    last = reduce_done(2, 1, fbuf)
    inside = (iota((8, 128), 1) >= 48) & (iota((8, 128), 1) < 64)
    gm[48:56, :] += jnp.where(inside, last, 0.0)
    gm[56:64, :] += jnp.where(inside, pltpu.roll(last, 112, 1), 0.0)
    lax.fori_loop(48, 64, eliminate, 0)

    c = [gm[16 * j : 16 * j + 16, :] for j in range(4)]
    half = 0.5 * delta
    unit = jnp.where(iota((16, 128), 0) == iota((16, 128), 1) - 64, 1.0, 0.0)
    e = [
        unit - theta * c[0] - half * c[1],
        -(theta * c[1] + delta * c[0] + half * c[2]),
        -(theta * c[2] + half * (c[1] + c[3])),
        -(theta * c[3] + half * c[2]),
        -(half * c[3]),
    ]
    nothing = jnp.zeros((16, 128), F32)
    forx = jnp.concatenate(c + [nothing] * 4, 0).T
    forr = jnp.concatenate(e + [nothing] * 3, 0).T
    coef = jnp.concatenate([forx[64:80], forr[64:80]], 0)
    spread_in = ones_where((iota((128, 640), 1) >> 3) == iota((128, 640), 0))
    spread_out = ones_where((iota((256, 32), 0) >> 3) == iota((256, 32), 1))
    same = (iota((256, 640), 0) & 7) == (iota((256, 640), 1) & 7)

    def wide(value):
        value = dot(spread_out, dot(value, spread_in).astype(BF))
        return jnp.where(same, value, 0.0).astype(BF)

    chigh, clow = split(coef)
    chigh, clow = wide(chigh), wide(clow)
    stores = []
    for pair in range(4):
        at = slice(256 * pair, 256 * pair + 256)
        high, low = fhigh[:, at], flow[:, at]
        out = dot(chigh, high) + dot(chigh, low) + dot(clow, high)
        for g in (2 * pair, 2 * pair + 1):
            one = out[:, 128 * (g - 2 * pair) : 128 * (g - 2 * pair) + 128]
            xo[:, :, 8 * g : 8 * g + 8, :] = x0[:, :, 8 * g : 8 * g + 8, :] + one[0:128].reshape(NQ, CQ, 8, 128)
            ro[:, :, 8 * g : 8 * g + 8, :] = one[128:256].reshape(NQ, CQ, 8, 128)
        rows = pl.ds(16 * pair, 16)
        for n, (src, dst) in enumerate(((xo, xo_out), (ro, ro_out))):
            stores.append(pltpu.make_async_copy(src.at[:, :, rows, :], dst.at[:, :, rows, :], outs.at[n, pair]))
            stores[-1].start()

    for q in range(NQ):
        return_sent(q)
    for store in stores:
        store.wait()


def on_device(start_block, labels, materials, mat_scales, cell_stiffness):
    nx, ny = lax.axis_size("gx"), lax.axis_size("gy")
    slots = 8 + ny // 4 + nx // 2
    block = jax.ShapeDtypeStruct((NQ, CQ, 64, 128), F32)
    out = pl.pallas_call(
        functools.partial(kernel, nx, ny),
        out_shape=[block, block],
        in_specs=[pl.BlockSpec(memory_space=pltpu.HBM)] * 7,
        out_specs=[pl.BlockSpec(memory_space=pltpu.HBM)] * 2,
        scratch_shapes=[
            pltpu.VMEM((NQ, CQ, 64, 128), F32),
            pltpu.VMEM((NQ, CQ, 64, 128), F32),
            pltpu.VMEM((NQ, CQ, 64, 128), F32),
            pltpu.VMEM((64, 128), jnp.int32),
            pltpu.VMEM((1, 128), jnp.int32),
            pltpu.SMEM((8,), F32),
            pltpu.VMEM((125, 125), F32),
            pltpu.VMEM((128, 128), BF),
            pltpu.VMEM((128, 1536), BF),
            pltpu.VMEM((5, NQ, CQ, 64, 128), F32),
            pltpu.VMEM((NQ, CQ, 64, 128), F32),
            pltpu.VMEM((NQ, CQ, 32, 128), F32),
            pltpu.VMEM((NQ, 4 * CQ, 128), F32),
            pltpu.VMEM((NQ, CQ, 16, 128), F32),
            pltpu.VMEM((NQ, 4 * CQ, 128), F32),
            pltpu.VMEM((NQ, CQ, 32, 128), F32),
            pltpu.VMEM((NQ, 4 * CQ, 128), F32),
            pltpu.VMEM((NQ, CQ, 32, 128), F32),
            pltpu.VMEM((NQ, 4 * CQ, 128), F32),
            pltpu.VMEM((NQ, CQ, 8, 128), F32),
            pltpu.VMEM((NQ, CQ, 8, 128), F32),
            pltpu.VMEM((128, 128), F32),
            pltpu.VMEM((128, 256), BF),
            pltpu.VMEM((128, 128), BF),
            pltpu.VMEM((64, 128), F32),
            pltpu.VMEM((8, 128), F32),
            pltpu.VMEM((slots, 16, 128), F32),
            pltpu.VMEM((slots, 8, 128), F32),
            pltpu.VMEM((64, 128), F32),
            pltpu.VMEM((256, 1024), BF),
            pltpu.VMEM((16, 128), F32),
            pltpu.VMEM((8, 128), F32),
            pltpu.VMEM((640, 1024), BF),
            pltpu.VMEM((640, 1024), BF),
            pltpu.SemaphoreType.DMA((3, NQ)),
            pltpu.SemaphoreType.DMA((3, NQ)),
            pltpu.SemaphoreType.DMA((3, NQ)),
            pltpu.SemaphoreType.DMA((3, NQ)),
            pltpu.SemaphoreType.DMA((2, slots)),
            pltpu.SemaphoreType.DMA((2, slots)),
            pltpu.SemaphoreType.DMA((7,)),
            pltpu.SemaphoreType.DMA((2, 4)),
        ],
        compiler_params=pltpu.CompilerParams(
            collective_id=0, has_side_effects=True, vmem_limit_bytes=56 * 1024 * 1024
        ),
    )(
        start_block.reshape(NQ, CQ, 64, 128),
        labels.reshape(64, 128),
        materials.reshape(1, 128),
        mat_scales,
        cell_stiffness,
        jnp.asarray(order_matrix()),
        jnp.asarray(moment_tables()),
    )
    return tuple(one.reshape(start_block.shape) for one in out)


def solution(mesh):
    spread = P(None, "gx", "gy", None, None)
    return jax.shard_map(
        on_device,
        mesh=mesh,
        in_specs=(spread, P("gx", "gy", None, None), P("gx", "gy", None), P(), P()),
        out_specs=(spread, spread),
        check_vma=False,
    )
```

```python
import functools

import jax
import jax.numpy as jnp
import ml_dtypes
import numpy as np
from jax import lax
from jax.experimental import pallas as pl
from jax.experimental.pallas import tpu as pltpu
from jax.sharding import PartitionSpec as P

COLS = 16
NQ = 8
CQ = COLS // NQ
PENALTY = 1.0
MESH = pl.DeviceIdType.MESH
BF = jnp.bfloat16
F32 = jnp.float32


def node_order():
    rows = [(a, b, d) for a in range(4) for b in range(4) for d in range(4)]
    rows += [(4, b, d) for b in range(4) for d in range(4)]
    rows += [(a, 4, d) for a in range(4) for d in range(4)]
    rows += [(a, b, 4) for a in range(4) for b in range(4)]
    rows += [(4, b, 4) for b in range(4)]
    rows += [(a, 4, 4) for a in range(4)]
    rows += [(4, 4, d) for d in range(5)]
    return [25 * a + 5 * b + d for a, b, d in rows]


def order_matrix():
    out = np.zeros((128, 128), np.float32)
    for row, node in enumerate(node_order()):
        out[row, node] = 1.0
    return out.astype(ml_dtypes.bfloat16)


def moment_tables():
    mu = np.zeros((7, 8))
    for k in range(3):
        mu[k, 4 + k] = 1.0
    mu[3, 0] = 1.0
    for i in (1, 2, 3):
        mu[3 + i, i] = 2.0
        mu[3 + i] -= mu[3 - i]

    def inner(i, j):
        return 0.5 * (mu[i + j] + mu[abs(i - j)])

    tables = np.zeros((3, 4, 8, 8))
    for i in range(4):
        for j in range(4):
            if i + j < 6:
                tables[0, i, :, j] = inner(i, j)
                tables[1, i, :, j] = 0.5 * (inner(i, j + 1) + inner(i, abs(j - 1)))
        tables[2, i, :, 4] = inner(i, 0)
    out = np.zeros((128, 3 * 4 * 128), np.float32)
    for which in range(3):
        for i in range(4):
            start = 128 * (4 * which + i)
            out[:, start : start + 128] = np.kron(tables[which, i], np.eye(16))
    return out.astype(ml_dtypes.bfloat16)


def split(value):
    high = value.astype(BF)
    low = (value - high.astype(F32)).astype(BF)
    return high, low


def dot(left, right):
    return jnp.dot(left, right, preferred_element_type=F32)


def dot_t(left, right):
    return lax.dot_general(left, right, (((1,), (1,)), ((), ())), preferred_element_type=F32)


def exact_dot(value, table):
    rows = value.shape[0]
    high = value.astype(BF)
    rest = value - high.astype(F32)
    middle = rest.astype(BF)
    low = (rest - middle.astype(F32)).astype(BF)
    out = dot(jnp.concatenate([high, middle, low], 0), table)
    return out[0:rows] + out[rows : 2 * rows] + out[2 * rows : 3 * rows]


def iota(shape, axis):
    return lax.broadcasted_iota(jnp.int32, shape, axis)


def ones_where(condition):
    return jnp.where(condition, 1.0, 0.0).astype(BF)


def kernel(
    nx, ny,
    x0_in, lab_in, mat_in, ms_in, kin_in, order_in, table_in,
    xo_out, ro_out,
    xo, ro, x0, lab, mat, ms, kin, order, table,
    v, w, rim, corner, ysend, csend, zs, zcs, zr, zcr, tail, zct, kpad, kk, klo, maskb, srow,
    gbuf, fbuf, gm, yst, gres, colr, fhigh, flow,
    es, er, rs, rr, ss, sr, ins, outs,
):
    fetches = [
        pltpu.make_async_copy(src, dst, ins.at[n])
        for n, (src, dst) in enumerate(
            ((x0_in, x0), (kin_in, kin), (order_in, order), (ms_in, ms), (lab_in, lab), (mat_in, mat), (table_in, table))
        )
    ]
    for fetch in fetches:
        fetch.start()

    gx = lax.axis_index("gx")
    gy = lax.axis_index("gy")
    xprev = lax.rem(gx + nx - 1, nx)
    xnext = lax.rem(gx + 1, nx)
    has_prev = gy > 0
    has_next = gy < ny - 1
    yprev = lax.max(gy - 1, 0)
    ynext = lax.min(gy + 1, ny - 1)

    half = ny // 2
    nz = half // 2
    nxx = nx // 4
    y_lo, x_hi = lax.rem(gx, 4), lax.div(gx, 4)
    y_hi, in_half = lax.div(gy, half), lax.rem(gy, half)
    z, core = lax.div(in_half, 2), lax.rem(in_half, 2)
    stages = (
        (0, 2 * nxx, 2 * x_hi + core, lambda p: (4 * lax.div(p, 2) + y_lo, half * y_hi + 2 * z + lax.rem(p, 2))),
        (2 * nxx, nz, z, lambda p: (gx, half * y_hi + 2 * p + core)),
        (2 * nxx + nz, 8, 4 * y_hi + y_lo, lambda p: (4 * x_hi + lax.rem(p, 4), half * lax.div(p, 4) + in_half)),
    )

    barrier = pltpu.get_barrier_semaphore()

    def greet(device):
        pl.semaphore_signal(barrier, inc=1, device_id=device, device_id_type=MESH)

    greet((xprev, gy))
    greet((xnext, gy))

    @pl.when(has_prev)
    def _():
        greet((gx, yprev))
        greet((xprev, yprev))

    @pl.when(has_next)
    def _():
        greet((gx, ynext))
        greet((xnext, ynext))

    for _, size, pos, device in stages:
        def hello(i, carry, size=size, pos=pos, device=device):
            greet(device(lax.rem(pos + i, size)))
            return carry

        lax.fori_loop(1, size, hello, 0)

    kpad[...] = jnp.zeros_like(kpad)
    zct[...] = jnp.zeros_like(zct)
    tail[...] = jnp.zeros_like(tail)
    for fetch in fetches:
        fetch.wait()
    kpad[0:125, 0:125] = kin[...]
    khigh, klow = split(kpad[...])
    pm = order[...]

    def permuted(value):
        return dot_t(dot(pm, value).astype(BF), pm).astype(BF)

    khigh = permuted(khigh)
    kk[:, 0:128] = khigh
    kk[:, 128:256] = khigh
    klo[...] = permuted(klow)
    maskb[...] = jnp.where(lab[...] >= 0, PENALTY, 0.0)
    scale = jnp.zeros((1, 128), F32)
    largest = jnp.zeros((1, 128), F32)
    for which in range(8):
        scale = scale + jnp.where(mat[...] == which, ms[which], 0.0)
        largest = jnp.maximum(largest, jnp.full((1, 128), ms[which], F32))
    srow[...] = jnp.broadcast_to(scale, (8, 128))

    def total(value):
        return jnp.sum(jnp.sum(value, 0, keepdims=True), 1, keepdims=True)

    size = jnp.sqrt(jnp.maximum(total(kpad[...] * kpad[...]), 1e-30))
    unit_k = (kpad[...] / size).astype(BF)
    squared = dot(unit_k, unit_k).astype(BF)
    fourth = dot(squared, squared)
    top = size * jnp.sqrt(jnp.sqrt(jnp.sqrt(total(fourth * fourth))))
    top = PENALTY + largest * top
    colr[0:1, :] = 0.6 * top
    colr[1:2, :] = 0.35 * top
    colr[2:3, :] = 1.0 / (0.35 * top)

    @pl.when(jnp.logical_not(has_next))
    def _():
        rim[:, :, 16:32, :] = jnp.zeros((NQ, CQ, 16, 128), F32)
        corner[...] = jnp.zeros_like(corner)

    @pl.when(jnp.logical_not(has_prev))
    def _():
        zr[:, :, 16:32, :] = jnp.zeros((NQ, CQ, 16, 128), F32)
        zcr[...] = jnp.zeros_like(zcr)

    def rcopy(src, dst, send, recv, device):
        return pltpu.make_async_remote_copy(
            src_ref=src, dst_ref=dst, send_sem=send, recv_sem=recv, device_id=device, device_id_type=MESH
        )

    def ext(src, q):
        first = pl.ds(0, 16)
        return (
            rcopy(src.at[q, :, first], rim.at[q, :, first], es.at[0, q], er.at[0, q], (xprev, gy)),
            rcopy(ysend.at[q], rim.at[q, :, pl.ds(16, 16)], es.at[1, q], er.at[1, q], (gx, yprev)),
            rcopy(csend.at[q], corner.at[q], es.at[2, q], er.at[2, q], (xprev, yprev)),
        )

    def ret(q):
        first, second = pl.ds(0, 16), pl.ds(16, 16)
        return (
            rcopy(zs.at[q, :, first], zr.at[q, :, first], rs.at[0, q], rr.at[0, q], (xnext, gy)),
            rcopy(zs.at[q, :, second], zr.at[q, :, second], rs.at[1, q], rr.at[1, q], (gx, ynext)),
            rcopy(zcs.at[q], zcr.at[q], rs.at[2, q], rr.at[2, q], (xnext, ynext)),
        )

    def extend_start(src, q):
        for j in range(CQ):
            for a in range(4):
                ysend[q, j, 4 * a : 4 * a + 4, :] = src[q, j, 16 * a : 16 * a + 4, :]
            csend[q, 4 * j : 4 * j + 4, :] = src[q, j, 0:4, :]
        copies = ext(src, q)

        @pl.when(has_prev)
        def _():
            copies[2].start()
            copies[1].start()

        copies[0].start()

    def extend_arrived(src, q):
        copies = ext(src, q)
        copies[0].wait_recv()

        @pl.when(has_next)
        def _():
            copies[1].wait_recv()
            copies[2].wait_recv()

    def extend_sent(src, q):
        copies = ext(src, q)
        copies[0].wait_send()

        @pl.when(has_prev)
        def _():
            copies[1].wait_send()
            copies[2].wait_send()

    def return_start(q):
        copies = ret(q)

        @pl.when(has_next)
        def _():
            copies[2].start()
            copies[1].start()

        copies[0].start()

    def return_arrived(q):
        copies = ret(q)
        copies[0].wait_recv()

        @pl.when(has_prev)
        def _():
            copies[1].wait_recv()
            copies[2].wait_recv()

    def return_sent(q):
        copies = ret(q)
        copies[0].wait_send()

        @pl.when(has_next)
        def _():
            copies[1].wait_send()
            copies[2].wait_send()

    def next_plane(value):
        lane = iota(value.shape, 1)
        return jnp.where(lane == 127, 0.0, pltpu.roll(value, 127, 1))

    def prev_plane(value):
        lane = iota(value.shape, 1)
        return jnp.where(lane == 0, 0.0, pltpu.roll(value, 1, 1))

    def cells(src, q):
        blocks = []
        for j in range(CQ):
            tail[q, j, 0:4, :] = corner[q, 4 * j : 4 * j + 4, :]
            tail[q, j, 4:5, :] = next_plane(corner[q, 4 * j : 4 * j + 1, :])
            blocks.append(
                jnp.concatenate(
                    [
                        src[q, j],
                        rim[q, j],
                        next_plane(src[q, j, pl.ds(0, 16, stride=4), :]),
                        next_plane(rim[q, j, pl.ds(0, 8, stride=4), :]),
                        tail[q, j],
                    ],
                    0,
                )
            )
        high, low = split(jnp.concatenate(blocks, 1))
        mapped = dot(kk[...], jnp.concatenate([high, low], 0)) + dot(klo[...], high)
        scales = srow[0:1, :]
        for j in range(CQ):
            out = mapped[:, 128 * j : 128 * j + 128] * scales
            w[q, j] = out[0:64] + maskb[...] * src[q, j]
            w[q, j, pl.ds(0, 16, stride=4), :] += prev_plane(out[96:112])
            zs[q, j] = out[64:96]
            zs[q, j, pl.ds(0, 8, stride=4), :] += prev_plane(out[112:120])
            zct[q, j, 0:4, :] = out[120:124]
            zct[q, j, 0:1, :] += prev_plane(out[124:125])
            zcs[q, 4 * j : 4 * j + 4, :] = zct[q, j, 0:4, :]

    def gather_rims(q):
        for j in range(CQ):
            w[q, j, 0:16, :] += zr[q, j, 0:16, :]
            for a in range(4):
                w[q, j, 16 * a : 16 * a + 4, :] += zr[q, j, 16 + 4 * a : 20 + 4 * a, :]
            w[q, j, 0:4, :] += zcr[q, 4 * j : 4 * j + 4, :]

    def operate(src, number, finish, target, between=None, after=None):
        lag = NQ - 4

        def apply(q):
            extend_arrived(src, q)
            if number > 0:
                return_sent(q)
            cells(src, q)
            return_start(q)

        def done(q):
            return_arrived(q)
            extend_sent(src, q)
            gather_rims(q)
            finish(q)
            if target is not None:
                extend_start(target, q)

        def lead(q, carry):
            apply(q)
            return carry

        def both(q, carry):
            apply(q)
            done(q - lag)
            return carry

        def trail(q, carry):
            done(q)
            return carry

        lax.fori_loop(0, lag, lead, 0)
        if between is None:
            lax.fori_loop(lag, NQ, both, 0)
            lax.fori_loop(NQ - lag, NQ, trail, 0)
        else:
            between()
            lax.fori_loop(lag, NQ, lead, 0)
            after()
            lax.fori_loop(0, NQ, trail, 0)

    def reduce_start(stage, number, buf, value):
        start, size, pos, device = stages[stage]
        buf[start + pos] = value

        def send(i, carry):
            p = lax.rem(pos + i, size)
            here = buf.at[start + pos]
            rcopy(here, here, ss.at[number, start + p], sr.at[number, start + pos], device(p)).start()
            return carry

        lax.fori_loop(1, size, send, 0)

    def reduce_done(stage, number, buf):
        start, size, pos, device = stages[stage]

        def take(i, carry):
            p = lax.rem(pos + i, size)
            here = buf.at[start + p]
            copy = rcopy(here, here, ss.at[number, start + p], sr.at[number, start + p], device(p))
            copy.wait_recv()
            copy.wait_send()
            return carry

        lax.fori_loop(1, size, take, 0)
        total = buf[start]
        for p in range(1, size):
            total = total + buf[start + p]
        return total

    pl.semaphore_wait(
        barrier,
        2 + 7 + (nz - 1) + (2 * nxx - 1) + 2 * (gy > 0).astype(jnp.int32) + 2 * (gy < ny - 1).astype(jnp.int32),
    )

    def first(q, carry):
        extend_start(x0, q)
        return carry

    lax.fori_loop(0, NQ, first, 0)

    def finish0(q):
        for j in range(CQ):
            target = jnp.where(lab[...] == CQ * q + j, 1.0, 0.0)
            v[0, q, j] = target - w[q, j]

    operate(x0, 0, finish0, v.at[0])

    def finish1(q):
        theta, inverse = colr[0:1, :], colr[2:3, :]
        for j in range(CQ):
            v[1, q, j] = (w[q, j] - theta * v[0, q, j]) * inverse

    operate(v.at[0], 1, finish1, v.at[1])

    def finish_next(number):
        def finish(q):
            theta, inverse = colr[0:1, :], colr[2:3, :]
            for j in range(CQ):
                v[number, q, j] = 2.0 * (w[q, j] - theta * v[number - 1, q, j]) * inverse - v[number - 2, q, j]

        return finish

    operate(v.at[1], 2, finish_next(2), v.at[2])

    def grouped(value):
        return [
            value[:, :, 8 * g : 8 * g + 8, :].reshape(8 * COLS, 128) for g in range(value.shape[2] // 8)
        ]

    def stacked(groups):
        high, low = split(jnp.concatenate(groups, 1))
        return jnp.concatenate([high, low], 0)

    def block(left, right):
        out = dot_t(left, right)
        out = out[0:128, 0:128] + out[0:128, 128:256] + out[128:256, 0:128] + out[128:256, 128:256]
        same = (iota((128, 128), 0) & 7) == (iota((128, 128), 1) & 7)
        return jnp.sum(jnp.where(same, out, 0.0).reshape(COLS, 8, 128), 1)

    def placed(value, lane):
        return exact_dot(value, ones_where(iota((128, 128), 1) == lane + (iota((128, 128), 0) >> 3)))

    def grams(number, count, offset):
        yst[...] = stacked(grouped(v[number]))

        def one(j, carry):
            gres[...] += placed(block(stacked(grouped(v[j])), yst[...]), 16 * (offset + j))
            return carry

        lax.fori_loop(0, count, one, 0)

    gres[...] = jnp.zeros_like(gres)
    grams(0, 3, 4)
    operate(v.at[2], 3, finish_next(3), v.at[3])
    grams(3, 4, 0)
    reduce_start(0, 0, gbuf, gres[...])

    def between():
        reduce_start(1, 0, gbuf, reduce_done(0, 0, gbuf))

    def after():
        last = block(
            stacked(grouped(v[3]) + grouped(rim[...]) + grouped(tail[...])),
            stacked(grouped(w[...]) + grouped(zs[...]) + grouped(zct[...])),
        )
        reduce_start(0, 1, fbuf, placed(last[0:8], 48) + placed(last[8:16], 64))
        reduce_start(2, 0, gbuf, reduce_done(1, 0, gbuf))
        reduce_start(1, 1, fbuf, reduce_done(0, 1, fbuf))

    operate(v.at[3], 4, finish_next(4), None, between, after)

    theta, delta = colr[0:1, :], colr[1:2, :]
    parts = exact_dot(reduce_done(2, 0, gbuf), table[...])
    for i in range(4):
        at = [parts[:, 128 * (4 * which + i) : 128 * (4 * which + i) + 128] for which in range(3)]
        gm[16 * i : 16 * i + 16, :] = theta * at[0] + delta * at[1] + at[2]

    def eliminate(k, carry):
        row = gm[pl.ds(k, 1), :]
        value = gm[...]
        here = iota((64, 128), 1) == k
        col = jnp.sum(jnp.where(here, value, 0.0), 1, keepdims=True)
        pivot = jnp.sum(jnp.where(iota((1, 128), 1) == k, row, 0.0), 1, keepdims=True)
        row = row / pivot
        gm[...] = jnp.where(iota((64, 128), 0) == k, row, value - col * row)
        return carry

    lax.fori_loop(0, 16, eliminate, 0)
    reduce_start(2, 1, fbuf, reduce_done(1, 1, fbuf))
    lax.fori_loop(16, 48, eliminate, 0)
    for j in range(5):
        high, low = split(jnp.concatenate(grouped(v[j]), 1))
        fhigh[128 * j : 128 * j + 128, :] = high
        flow[128 * j : 128 * j + 128, :] = low
    last = reduce_done(2, 1, fbuf)
    inside = (iota((8, 128), 1) >= 48) & (iota((8, 128), 1) < 64)
    gm[48:56, :] += jnp.where(inside, last, 0.0)
    gm[56:64, :] += jnp.where(inside, pltpu.roll(last, 112, 1), 0.0)
    lax.fori_loop(48, 64, eliminate, 0)

    c = [gm[16 * j : 16 * j + 16, :] for j in range(4)]
    half = 0.5 * delta
    unit = jnp.where(iota((16, 128), 0) == iota((16, 128), 1) - 64, 1.0, 0.0)
    e = [
        unit - theta * c[0] - half * c[1],
        -(theta * c[1] + delta * c[0] + half * c[2]),
        -(theta * c[2] + half * (c[1] + c[3])),
        -(theta * c[3] + half * c[2]),
        -(half * c[3]),
    ]
    nothing = jnp.zeros((16, 128), F32)
    forx = jnp.concatenate(c + [nothing] * 4, 0).T
    forr = jnp.concatenate(e + [nothing] * 3, 0).T
    coef = jnp.concatenate([forx[64:80], forr[64:80]], 0)
    spread_in = ones_where((iota((128, 640), 1) >> 3) == iota((128, 640), 0))
    spread_out = ones_where((iota((256, 32), 0) >> 3) == iota((256, 32), 1))
    same = (iota((256, 640), 0) & 7) == (iota((256, 640), 1) & 7)

    def wide(value):
        value = dot(spread_out, dot(value, spread_in).astype(BF))
        return jnp.where(same, value, 0.0).astype(BF)

    chigh, clow = split(coef)
    chigh, clow = wide(chigh), wide(clow)
    cboth = jnp.concatenate([chigh, clow], 0)
    stores = []
    for pair in range(4):
        at = slice(256 * pair, 256 * pair + 256)
        high, low = fhigh[:, at], flow[:, at]
        both = dot(cboth, high)
        out = both[0:256] + both[256:512] + dot(chigh, low)
        for g in (2 * pair, 2 * pair + 1):
            one = out[:, 128 * (g - 2 * pair) : 128 * (g - 2 * pair) + 128]
            xo[:, :, 8 * g : 8 * g + 8, :] = x0[:, :, 8 * g : 8 * g + 8, :] + one[0:128].reshape(NQ, CQ, 8, 128)
            ro[:, :, 8 * g : 8 * g + 8, :] = one[128:256].reshape(NQ, CQ, 8, 128)
        rows = pl.ds(16 * pair, 16)
        for n, (src, dst) in enumerate(((xo, xo_out), (ro, ro_out))):
            stores.append(pltpu.make_async_copy(src.at[:, :, rows, :], dst.at[:, :, rows, :], outs.at[n, pair]))
            stores[-1].start()

    for q in range(NQ):
        return_sent(q)
    for store in stores:
        store.wait()


def on_device(start_block, labels, materials, mat_scales, cell_stiffness):
    nx, ny = lax.axis_size("gx"), lax.axis_size("gy")
    slots = 8 + ny // 4 + nx // 2
    block = jax.ShapeDtypeStruct((NQ, CQ, 64, 128), F32)
    out = pl.pallas_call(
        functools.partial(kernel, nx, ny),
        out_shape=[block, block],
        in_specs=[pl.BlockSpec(memory_space=pltpu.HBM)] * 7,
        out_specs=[pl.BlockSpec(memory_space=pltpu.HBM)] * 2,
        scratch_shapes=[
            pltpu.VMEM((NQ, CQ, 64, 128), F32),
            pltpu.VMEM((NQ, CQ, 64, 128), F32),
            pltpu.VMEM((NQ, CQ, 64, 128), F32),
            pltpu.VMEM((64, 128), jnp.int32),
            pltpu.VMEM((1, 128), jnp.int32),
            pltpu.SMEM((8,), F32),
            pltpu.VMEM((125, 125), F32),
            pltpu.VMEM((128, 128), BF),
            pltpu.VMEM((128, 1536), BF),
            pltpu.VMEM((5, NQ, CQ, 64, 128), F32),
            pltpu.VMEM((NQ, CQ, 64, 128), F32),
            pltpu.VMEM((NQ, CQ, 32, 128), F32),
            pltpu.VMEM((NQ, 4 * CQ, 128), F32),
            pltpu.VMEM((NQ, CQ, 16, 128), F32),
            pltpu.VMEM((NQ, 4 * CQ, 128), F32),
            pltpu.VMEM((NQ, CQ, 32, 128), F32),
            pltpu.VMEM((NQ, 4 * CQ, 128), F32),
            pltpu.VMEM((NQ, CQ, 32, 128), F32),
            pltpu.VMEM((NQ, 4 * CQ, 128), F32),
            pltpu.VMEM((NQ, CQ, 8, 128), F32),
            pltpu.VMEM((NQ, CQ, 8, 128), F32),
            pltpu.VMEM((128, 128), F32),
            pltpu.VMEM((128, 256), BF),
            pltpu.VMEM((128, 128), BF),
            pltpu.VMEM((64, 128), F32),
            pltpu.VMEM((8, 128), F32),
            pltpu.VMEM((slots, 16, 128), F32),
            pltpu.VMEM((slots, 8, 128), F32),
            pltpu.VMEM((64, 128), F32),
            pltpu.VMEM((256, 1024), BF),
            pltpu.VMEM((16, 128), F32),
            pltpu.VMEM((8, 128), F32),
            pltpu.VMEM((640, 1024), BF),
            pltpu.VMEM((640, 1024), BF),
            pltpu.SemaphoreType.DMA((3, NQ)),
            pltpu.SemaphoreType.DMA((3, NQ)),
            pltpu.SemaphoreType.DMA((3, NQ)),
            pltpu.SemaphoreType.DMA((3, NQ)),
            pltpu.SemaphoreType.DMA((2, slots)),
            pltpu.SemaphoreType.DMA((2, slots)),
            pltpu.SemaphoreType.DMA((7,)),
            pltpu.SemaphoreType.DMA((2, 4)),
        ],
        compiler_params=pltpu.CompilerParams(
            collective_id=0, has_side_effects=True, vmem_limit_bytes=56 * 1024 * 1024
        ),
    )(
        start_block.reshape(NQ, CQ, 64, 128),
        labels.reshape(64, 128),
        materials.reshape(1, 128),
        mat_scales,
        cell_stiffness,
        jnp.asarray(order_matrix()),
        jnp.asarray(moment_tables()),
    )
    return tuple(one.reshape(start_block.shape) for one in out)


def solution(mesh):
    spread = P(None, "gx", "gy", None, None)
    return jax.shard_map(
        on_device,
        mesh=mesh,
        in_specs=(spread, P("gx", "gy", None, None), P("gx", "gy", None), P(), P()),
        out_specs=(spread, spread),
        check_vma=False,
    )
```
